256 devices in a mesh: batch: 16 (over z, core), feat: 16 (over y, x).
Axes of the slice: x: 4, y: 4, z: 8, core: 2. Of those that a mesh axis runs over, the one named last changes fastest.
Arguments:
- noise: bfloat16 [128, 1048576], P('batch', 'feat'), may hold values from -7 to 7
- data: bfloat16 [128, 1048576], P('batch', 'feat'), may hold values from -5 to 5
Outputs:
- targets: bfloat16 [128, 1048576], P('batch', 'feat')
- row_potential: float32 [128], P('batch')
- column_potential: float32 [128], replicated
The draws below stay inside these ranges and needn't reach their ends.
All inputs are finite; a program needn't handle non-finite values.
Results may differ from the reference program's by a relative error of at most 0.012.
Values may be sent and summed in bfloat16 or wider, within the bound.
A program may use at most 64 MiB of HBM per device.

```python
import math
import jax
import jax.numpy as jnp
from jax import lax

F = 1048576
ITERS = 3
B = 128


def draw_noise(key, part):
    key = jax.random.fold_in(key, 11)
    value_key, scale_key = jax.random.split(key)
    values = jnp.clip(jax.random.normal(value_key, (B, F), jnp.float32), -5.0, 5.0)
    scales = jnp.exp(jax.random.uniform(scale_key, (B, 1), jnp.float32, math.log(0.7), math.log(1.4)))
    return (values * scales).astype(jnp.bfloat16)


def block_levels(key, extent, pieces, low, largest):
    factor_of, own = 1.0, jax.random.fold_in(key, 6)
    for axis_at, shards_of in pieces:
        heights = jnp.exp(jax.random.uniform(jax.random.fold_in(own, axis_at), (shards_of,), jnp.float32, low / len(pieces), largest / len(pieces)))
        factor_of = factor_of * jnp.repeat(heights, extent[axis_at] // shards_of).reshape([-1 if axis == axis_at else 1 for axis in range(len(extent))])
    return factor_of


def bell_draw(rng, extent, width, bound, shards=(), kind=jnp.bfloat16):
    result = jax.random.normal(rng, extent, jnp.float32) * width
    if len(shards) > 0:
        result = block_levels(rng, extent, shards, -0.22, 0.18) * result
    return jnp.clip(result, min=-bound, max=bound).astype(kind)


def setup_inputs(seed: int = 0) -> dict:
    arg_keys = jax.random.split(jax.random.key(seed), 3)
    return {
        "noise": draw_noise(jax.random.fold_in(arg_keys[2], 71), 0),
        "data": bell_draw(arg_keys[1], (B, F), 1.0, 5.0, ((0, 16), (1, 16))),
    }


def row_lse(values, axis):
    top = lax.optimization_barrier(jnp.max(values, axis=axis, keepdims=True))
    return jnp.squeeze(top, axis) + jnp.log(lax.optimization_barrier(jnp.sum(jnp.exp(values - top), axis=axis)))

def reference(noise, data):
    noise_norm = lax.optimization_barrier(jnp.sum(jnp.square(noise.astype(jnp.float32)), axis=1))
    data_norm = lax.optimization_barrier(jnp.sum(jnp.square(data.astype(jnp.float32)), axis=1))
    cross = jnp.dot(noise, data.T, preferred_element_type=jnp.float32)
    root = math.sqrt(F)
    scores = (2.0 * cross - noise_norm[:, None] - data_norm[None, :]) / root + 2.0 * root
    log_count = math.log(B)
    row_potential = jnp.zeros((B,), jnp.float32)
    column_potential = jnp.zeros((B,), jnp.float32)
    for step in range(ITERS):
        row_potential = -log_count - row_lse(scores + column_potential[None, :], 1)
        column_potential = -log_count - row_lse(scores + row_potential[:, None], 0)
    plan = jnp.exp(scores + row_potential[:, None] + column_potential[None, :])
    weights = (plan / lax.optimization_barrier(jnp.sum(plan, axis=1, keepdims=True))).astype(jnp.bfloat16)
    targets = jnp.dot(weights, data, preferred_element_type=jnp.float32).astype(jnp.bfloat16)
    return (targets, row_potential, column_potential)
```

```python
import functools
import math

import jax
import jax.numpy as jnp
from jax import lax
from jax.experimental import pallas as pl
from jax.experimental.pallas import tpu as pltpu
from jax.sharding import PartitionSpec as P

ITERS = 3
MESH = pl.DeviceIdType.MESH


def lse(values, axis):
    top = jnp.max(values, axis=axis, keepdims=True)
    return top + jnp.log(jnp.sum(jnp.exp(values - top), axis=axis, keepdims=True))


def ring_order(count):
    offsets = sorted(range(1, count), key=lambda k: (-min(k, count - k), k))
    return offsets


def kernel(
    nb, nf, noise, data, out, row_out, col_out,
    noise_buf, data_buf, local_buf, full, obuf, part, own, a_buf, b_buf, c_buf,
    norm_own, norm_b, norm_c, pot,
    local_sem, send_sem, recv_sem, small_send, small_recv, out_send, out_recv,
):
    rows, width = noise.shape
    w = width // nb
    total = rows * nb
    features = width * nf
    root = math.sqrt(features)
    log_count = math.log(total)
    b, f = lax.axis_index("batch"), lax.axis_index("feat")
    b_order, f_order = ring_order(nb), list(range(1, nf))

    def in_column(k):
        return dict(device_id=(lax.rem(b + k, nb), f), device_id_type=MESH)

    def in_plane(k):
        return dict(device_id=(b, lax.rem(f + k, nf)), device_id_type=MESH)

    def drain(ref, sem, count):
        view = ref.at[pl.ds(0, count)]
        pltpu.make_async_copy(view, view, sem).wait()

    barrier = pltpu.get_barrier_semaphore()
    for k in b_order:
        pl.semaphore_signal(barrier, inc=1, **in_column(k))
    for k in f_order:
        pl.semaphore_signal(barrier, inc=1, **in_plane(k))
    pl.semaphore_wait(barrier, nb + nf - 2)

    for k in b_order:
        t = lax.rem(b + k, nb)
        columns = pl.ds(pl.multiple_of(t * w, w), w)
        for i, (ref, buf) in enumerate(((noise, noise_buf), (data, data_buf))):
            pltpu.make_async_remote_copy(
                src_ref=ref.at[:, columns], dst_ref=buf.at[b],
                send_sem=send_sem.at[i], recv_sem=recv_sem.at[i], **in_column(k)
            ).start()
    mine = pl.ds(pl.multiple_of(b * w, w), w)
    locals_ = [
        pltpu.make_async_copy(noise, local_buf.at[0], local_sem.at[0]),
        pltpu.make_async_copy(data, local_buf.at[1], local_sem.at[1]),
        pltpu.make_async_copy(noise.at[:, mine], noise_buf.at[b], local_sem.at[2]),
        pltpu.make_async_copy(data.at[:, mine], data_buf.at[b], local_sem.at[3]),
    ]
    for c in locals_:
        c.start()
    for c in locals_:
        c.wait()

    def exchange(src_of, buf, slot, partner, order, sem):
        for k in order:
            pltpu.make_async_remote_copy(
                src_ref=src_of(k), dst_ref=buf.at[slot],
                send_sem=small_send.at[sem], recv_sem=small_recv.at[sem], **partner(k)
            ).start()

    chunk = min(2048, width)
    for i in range(2):
        def add(step, acc, i=i):
            v = local_buf[i, :, pl.ds(pl.multiple_of(step * chunk, chunk), chunk)].astype(jnp.float32)
            v = v * v
            for q in range(chunk // 128):
                acc = acc + v[:, q * 128:(q + 1) * 128]
            return acc
        acc = lax.fori_loop(0, width // chunk, add, jnp.zeros((rows, 128), jnp.float32))
        norm_own[0, i * rows:(i + 1) * rows, :] = jnp.broadcast_to(
            jnp.sum(acc, axis=1, keepdims=True), (rows, 128)
        )
    norm_b[f] = norm_own[0]
    exchange(lambda k: norm_own.at[0], norm_b, f, in_plane, f_order, 0)
    drain(norm_b, small_recv.at[0], nf - 1)
    norm_c[b] = jnp.sum(norm_b[...], axis=0)
    norm_own[1] = norm_c[b]
    exchange(lambda k: norm_own.at[1], norm_c, b, in_column, b_order, 1)
    drain(norm_c, small_recv.at[1], nb - 1)
    norms = norm_c[...]
    noise_norm = norms[:, :rows, :].reshape(total, 128)[:, :1]
    data_norm = norms[:, rows:, :].reshape(total, 128)
    data_norm = jnp.transpose(data_norm)[:1, :]

    drain(noise_buf, recv_sem.at[0], nb - 1)
    drain(data_buf, recv_sem.at[1], nb - 1)
    acc = jnp.zeros((total, total), jnp.float32)
    chunk = min(1024, w)
    for q in range(w // chunk):
        columns = pl.ds(q * chunk, chunk)
        left = noise_buf[:, :, columns].astype(jnp.float32).reshape(total, chunk).astype(jnp.bfloat16)
        right = data_buf[:, :, columns].astype(jnp.float32).reshape(total, chunk).astype(jnp.bfloat16)
        full[:, columns] = right
        acc = acc + lax.dot_general(
            left, right, (((1,), (1,)), ((), ())), preferred_element_type=jnp.float32
        )
    part[...] = acc.reshape(nb, rows, total)

    a_buf[b] = part[b]
    exchange(lambda k: part.at[lax.rem(b + k, nb)], a_buf, b, in_column, b_order, 2)
    drain(a_buf, small_recv.at[2], nb - 1)
    own[0] = jnp.sum(a_buf[...], axis=0)
    b_buf[f] = own[0]
    exchange(lambda k: own.at[0], b_buf, f, in_plane, f_order, 3)
    drain(b_buf, small_recv.at[3], nf - 1)
    own[1] = jnp.sum(b_buf[...], axis=0)
    c_buf[b] = own[1]
    exchange(lambda k: own.at[1], c_buf, b, in_column, b_order, 4)
    drain(c_buf, small_recv.at[4], nb - 1)
    cross = c_buf[...].reshape(total, total)

    scores = (2.0 * cross - noise_norm - data_norm) / root + 2.0 * root
    column = jnp.zeros((1, total), jnp.float32)
    for _ in range(ITERS):
        row = -log_count - lse(scores + column, 1)
        column = -log_count - lse(scores + row, 0)
    plan = jnp.exp(scores + row + column)
    weights = (plan / jnp.sum(plan, axis=1, keepdims=True)).astype(jnp.bfloat16)

    col_out[...] = column
    pot[...] = jnp.broadcast_to(row, (total, 128)).reshape(nb, rows, 128)
    diagonal = lax.broadcasted_iota(jnp.int32, (rows, 128), 0) == lax.broadcasted_iota(
        jnp.int32, (rows, 128), 1
    )
    flat = jnp.sum(jnp.where(diagonal, pot[b], 0.0), axis=0, keepdims=True)
    row_out[...] = flat[:, :rows]

    groups = 2
    gw = w // groups
    for g in range(groups):
        step = min(512, gw)
        for q in range(gw // step):
            columns = pl.ds(g * gw + q * step, step)
            summed = jnp.dot(weights, full[:, columns], preferred_element_type=jnp.float32)
            obuf[g, :, :, q * step:(q + 1) * step] = summed.reshape(nb, rows, step).astype(jnp.bfloat16)
        here = pl.ds(pl.multiple_of(b * w + g * gw, gw), gw)
        for k in b_order:
            pltpu.make_async_remote_copy(
                src_ref=obuf.at[g, lax.rem(b + k, nb)], dst_ref=out.at[:, here],
                send_sem=out_send.at[g], recv_sem=out_recv.at[g], **in_column(k)
            ).start()
        pltpu.make_async_copy(obuf.at[g, b], out.at[:, here], local_sem.at[g]).start()

    drain(noise_buf, send_sem.at[0], nb - 1)
    drain(data_buf, send_sem.at[1], nb - 1)
    drain(norm_b, small_send.at[0], nf - 1)
    drain(norm_c, small_send.at[1], nb - 1)
    drain(a_buf, small_send.at[2], nb - 1)
    drain(b_buf, small_send.at[3], nf - 1)
    drain(c_buf, small_send.at[4], nb - 1)
    for g in range(groups):
        drain(obuf.at[g], out_send.at[g], nb - 1)
        drain(obuf.at[g], out_recv.at[g], nb - 1)
        pltpu.make_async_copy(
            obuf.at[g, b], out.at[:, pl.ds(pl.multiple_of(b * w + g * gw, gw), gw)], local_sem.at[g]
        ).wait()


def solution(mesh):
    nb, nf = mesh.shape["batch"], mesh.shape["feat"]

    def per_device(noise, data):
        rows, width = noise.shape
        total, w = rows * nb, width // nb
        targets, row, column = pl.pallas_call(
            functools.partial(kernel, nb, nf),
            out_shape=(
                jax.ShapeDtypeStruct((rows, width), jnp.bfloat16),
                jax.ShapeDtypeStruct((1, rows), jnp.float32),
                jax.ShapeDtypeStruct((1, total), jnp.float32),
            ),
            in_specs=[pl.BlockSpec(memory_space=pl.ANY)] * 2,
            out_specs=(
                pl.BlockSpec(memory_space=pl.ANY),
                pl.BlockSpec(memory_space=pltpu.VMEM),
                pl.BlockSpec(memory_space=pltpu.VMEM),
            ),
            scratch_shapes=[
                pltpu.VMEM((nb, rows, w), jnp.bfloat16),
                pltpu.VMEM((nb, rows, w), jnp.bfloat16),
                pltpu.VMEM((2, rows, width), jnp.bfloat16),
                pltpu.VMEM((total, w), jnp.bfloat16),
                pltpu.VMEM((2, nb, rows, w // 2), jnp.bfloat16),
                pltpu.VMEM((nb, rows, total), jnp.float32),
                pltpu.VMEM((2, rows, total), jnp.float32),
                pltpu.VMEM((nb, rows, total), jnp.float32),
                pltpu.VMEM((nf, rows, total), jnp.float32),
                pltpu.VMEM((nb, rows, total), jnp.float32),
                pltpu.VMEM((2, 2 * rows, 128), jnp.float32),
                pltpu.VMEM((nf, 2 * rows, 128), jnp.float32),
                pltpu.VMEM((nb, 2 * rows, 128), jnp.float32),
                pltpu.VMEM((nb, rows, 128), jnp.float32),
                pltpu.SemaphoreType.DMA((4,)),
                pltpu.SemaphoreType.DMA((2,)),
                pltpu.SemaphoreType.DMA((2,)),
                pltpu.SemaphoreType.DMA((5,)),
                pltpu.SemaphoreType.DMA((5,)),
                pltpu.SemaphoreType.DMA((2,)),
                pltpu.SemaphoreType.DMA((2,)),
            ],
            compiler_params=pltpu.CompilerParams(
                collective_id=0, has_side_effects=True, vmem_limit_bytes=56 * 2**20
            ),
        )(noise, data)
        return targets, row.reshape(rows), column.reshape(total)

    return jax.shard_map(
        per_device,
        mesh=mesh,
        in_specs=(P("batch", "feat"), P("batch", "feat")),
        out_specs=(P("batch", "feat"), P("batch"), P()),
        check_vma=False,
    )
```

```python
import functools
import math

import jax
import jax.numpy as jnp
from jax import lax
from jax.experimental import pallas as pl
from jax.experimental.pallas import tpu as pltpu
from jax.sharding import PartitionSpec as P

ITERS = 3
SHARED = 6
EARLY = 3
MESH = pl.DeviceIdType.MESH


def lse(values, axis):
    top = jnp.max(values, axis=axis, keepdims=True)
    return top + jnp.log(jnp.sum(jnp.exp(values - top), axis=axis, keepdims=True))


def far_first(count):
    return sorted(range(1, count), key=lambda k: (-min(k, count - k), k))


def kernel(
    nb, nf, noise, data, out, row_out, col_out,
    noise_buf, data_buf, outer_buf, full, outer_full, local_buf, obuf, outer_obuf, part, a_buf, own, b_buf, done, c_buf,
    norm_own, norm_b, pot, wbuf,
    local_sem, outer_send, outer_recv, first_send, first_recv, noise_send, noise_recv, on_send, on_recv,
    small_send, small_recv, out_send, out_recv,
):
    rows, width = noise.shape
    w = width // nb
    total = rows * nb
    piece = total // nf
    features = width * nf
    root = math.sqrt(features)
    log_count = math.log(total)
    half = nb // 4
    shared = w * SHARED // 8
    b, f = lax.axis_index("batch"), lax.axis_index("feat")
    core = lax.rem(b, 2)
    sibling = b + 1 - 2 * core
    b_order, f_order = far_first(nb), list(range(1, nf))

    def at(t):
        return dict(device_id=(t, f), device_id_type=MESH)

    def in_column(k):
        return at(lax.rem(b + k, nb))

    def in_plane(k):
        return dict(device_id=(b, lax.rem(f + k, nf)), device_id_type=MESH)

    def drain(ref, sem, count):
        view = ref.at[pl.ds(0, count)]
        pltpu.make_async_copy(view, view, sem).wait()

    def wrap(t):
        return lax.rem(t + 2 * nb, nb)

    def columns_of(slice_at, q=0, n=w):
        return pl.ds(pl.multiple_of(slice_at * w + q, math.gcd(w, q)), n)

    def step_of(role):
        return 2 if role == 0 else -2

    barrier = pltpu.get_barrier_semaphore()
    for k in b_order:
        pl.semaphore_signal(barrier, inc=1, **in_column(k))
    for k in f_order:
        pl.semaphore_signal(barrier, inc=1, **in_plane(k))
    pl.semaphore_wait(barrier, nb + nf - 2)

    def slice_for(role, member):
        return wrap(member - 2 * role)

    for role in range(2):
        for member in (b, sibling):
            pltpu.make_async_remote_copy(
                src_ref=data.at[:, columns_of(slice_for(role, member))], dst_ref=data_buf.at[1 - role, b],
                send_sem=on_send.at[role, 0], recv_sem=on_recv.at[1 - role, 0],
                **at(wrap(member + step_of(role)))
            ).start()
    for d in range(half - 1, -1, -1):
        for role in range(2):
            for member in ([wrap(sibling + step_of(role) * d)] if d == 0 else []) + (
                [wrap(b + step_of(role) * d), wrap(sibling + step_of(role) * d)] if d else []
            ):
                pltpu.make_async_remote_copy(
                    src_ref=data.at[:, columns_of(slice_for(role, member))], dst_ref=data_buf.at[role, b],
                    send_sem=first_send.at[role, d], recv_sem=first_recv.at[role, d], **at(member)
                ).start()
    locals_ = []
    for role in range(2):
        s = columns_of(slice_for(role, b))
        locals_.append(pltpu.make_async_copy(data.at[:, s], data_buf.at[role, b], local_sem.at[role]))
        locals_.append(pltpu.make_async_copy(noise.at[:, s], noise_buf.at[role, core], local_sem.at[2 + role]))
    locals_.append(pltpu.make_async_copy(noise, local_buf.at[0], local_sem.at[4]))
    locals_.append(pltpu.make_async_copy(data, local_buf.at[1], local_sem.at[5]))
    def outer_slice(role, device):
        return slice_for(role, wrap(device + step_of(role)))

    for role in range(2):
        s = columns_of(outer_slice(role, b), 0, shared)
        locals_.append(pltpu.make_async_copy(data.at[:, s], outer_buf.at[role, b], local_sem.at[6 + role]))
    for c in locals_:
        c.start()
    for role in range(2):
        pltpu.make_async_remote_copy(
            src_ref=data.at[:, columns_of(outer_slice(role, sibling), 0, shared)],
            dst_ref=outer_buf.at[role, b],
            send_sem=outer_send.at[role, 0], recv_sem=outer_recv.at[role, 0], **at(sibling)
        ).start()
    for d in range(half - 1, -1, -1):
        for role in range(2):
            for member in [sibling] if d == 0 else [
                wrap(b + step_of(role) * d), wrap(sibling + step_of(role) * d)
            ]:
                pltpu.make_async_remote_copy(
                    src_ref=noise.at[:, columns_of(slice_for(role, member))],
                    dst_ref=noise_buf.at[role, 2 * d + core],
                    send_sem=noise_send.at[role], recv_sem=noise_recv.at[role], **at(member)
                ).start()
    for c in locals_:
        c.wait()

    def exchange(src_of, buf, slot, partner, order, sem):
        for k in order:
            pltpu.make_async_remote_copy(
                src_ref=src_of(k), dst_ref=buf.at[slot],
                send_sem=small_send.at[sem], recv_sem=small_recv.at[sem], **partner(k)
            ).start()

    chunk = min(2048, width)
    sums = []
    for i in range(2):
        def add(step, acc, i=i):
            v = local_buf[i, :, pl.ds(pl.multiple_of(step * chunk, chunk), chunk)].astype(jnp.float32)
            v = v * v
            for q in range(chunk // 128):
                acc = acc + v[:, q * 128:(q + 1) * 128]
            return acc
        acc = lax.fori_loop(0, width // chunk, add, jnp.zeros((rows, 128), jnp.float32))
        sums.append(jnp.sum(acc, axis=1, keepdims=True))
    lane = lax.broadcasted_iota(jnp.int32, (rows, 128), 1)
    norm_own[...] = jnp.where(lane < 64, sums[0], sums[1])
    norm_b[f] = norm_own[...]
    exchange(lambda k: norm_own, norm_b, f, in_plane, f_order, 0)

    def pair(chip_of):
        return pl.ds(pl.multiple_of(wrap(chip_of) // 2 * 2, 2), 2)

    for d in range(half - 1, 0, -1):
        for role in range(2):
            drain(data_buf.at[role], first_recv.at[role, d], 2)
            block = pair(b - step_of(role) * d)
            pltpu.make_async_remote_copy(
                src_ref=data_buf.at[role, block], dst_ref=data_buf.at[1 - role, block],
                send_sem=on_send.at[role, d], recv_sem=on_recv.at[1 - role, d],
                **at(wrap(b + step_of(role)))
            ).start()
    for role in range(2):
        drain(data_buf.at[role], first_recv.at[role, 0], 1)

    drain(norm_b, small_recv.at[0], nf - 1)
    own[piece:, :] = jnp.sum(norm_b[...], axis=0)

    for role in range(2):
        drain(noise_buf.at[role], noise_recv.at[role], nb // 2 - 1)
    for d in range(half):
        for role in range(2):
            drain(data_buf.at[role], on_recv.at[role, d], 2)

    def share(offsets):
        for d in offsets:
            for role in range(2):
                block = pair(b + step_of(role) * d)
                pltpu.make_async_remote_copy(
                    src_ref=data_buf.at[role, block, :, pl.ds(0, shared)], dst_ref=outer_buf.at[role, block],
                    send_sem=outer_send.at[role, 1], recv_sem=outer_recv.at[role, 1],
                    **at(wrap(b - step_of(role)))
                ).start()

    onward = list(range(nb // 2 - 1))
    share(onward[:EARLY])

    acc = jnp.zeros((total, total), jnp.float32)
    chunk = min(1024, w)
    served = total // 2
    for q in range(w // chunk):
        columns = pl.ds(q * chunk, chunk)
        for role in range(2):
            left = data_buf[role, :, :, columns].astype(jnp.float32).reshape(total, chunk).astype(jnp.bfloat16)
            right = noise_buf[role, :, :, columns].astype(jnp.float32).reshape(served, chunk).astype(jnp.bfloat16)
            zero = jnp.zeros((served, chunk), jnp.bfloat16)
            right = jnp.concatenate([right, zero] if role == 0 else [zero, right], axis=0)
            acc = acc + lax.dot_general(
                left, right, (((1,), (1,)), ((), ())), preferred_element_type=jnp.float32
            )
    part[...] = acc.reshape(nf, total // nf, total)

    a_buf[f] = part[f]
    exchange(lambda k: part.at[lax.rem(f + k, nf)], a_buf, f, in_plane, f_order, 1)
    drain(a_buf, small_recv.at[1], nf - 1)
    mine = jnp.sum(a_buf[...], axis=0)
    lane = lax.broadcasted_iota(jnp.int32, mine.shape, 1)
    spread = jnp.zeros_like(mine)
    for d in range(half):
        for role in range(2):
            at_lane = role * served + d * 2 * rows
            chip = wrap(b - core - step_of(role) * d)
            group = jnp.where((lane >= at_lane) & (lane < at_lane + 2 * rows), mine, 0.0)
            spread = spread + pltpu.roll(group, lax.rem(chip * rows - at_lane + total, total), 1)
    own[:piece, :] = spread
    b_buf[b] = own[...]
    exchange(lambda k: own, b_buf, b, in_column, b_order, 2)
    share(onward[EARLY:])
    for role in range(2):
        for q in range(w // chunk):
            columns = pl.ds(q * chunk, chunk)
            full[role, :, columns] = (
                data_buf[role, :, :, columns].astype(jnp.float32).reshape(total, chunk).astype(jnp.bfloat16)
            )
    drain(b_buf, small_recv.at[2], nb - 1)
    done[...] = jnp.sum(b_buf[:, :piece, :], axis=0)
    c_buf[f] = done[...]
    exchange(lambda k: done, c_buf, f, in_plane, f_order, 3)
    norms = b_buf[:, piece:, :].reshape(total, 128)
    noise_norm = norms[:, :1]
    data_norm = jnp.transpose(norms)[64:65, :]
    drain(c_buf, small_recv.at[3], nf - 1)
    cross = jnp.transpose(c_buf[...].reshape(total, total))

    scores = (2.0 * cross - noise_norm - data_norm) / root + 2.0 * root
    column = jnp.zeros((1, total), jnp.float32)
    for _ in range(ITERS):
        row = -log_count - lse(scores + column, 1)
        column = -log_count - lse(scores + row, 0)
    plan = jnp.exp(scores + row + column)
    weights = plan / jnp.sum(plan, axis=1, keepdims=True)
    wbuf[...] = weights.reshape(nb, rows, total)

    step = min(512, shared)
    kept = []

    def targets(chips, role, values, buf, slice_at, first, count, sem):
        blocks = []
        for d in chips:
            blocks += [wrap(sibling - step_of(role) * d), wrap(b - step_of(role) * d)]
        chosen = jnp.concatenate([wbuf[t] for t in blocks], axis=0).astype(jnp.bfloat16)
        for q in range(0, count, step):
            n = min(step, count - q)
            summed = jnp.dot(chosen, values[role, :, first + q:first + q + n], preferred_element_type=jnp.float32)
            buf[role, :len(blocks), :, first + q:first + q + n] = summed.reshape(
                len(blocks), rows, n
            ).astype(jnp.bfloat16)
        where = columns_of(slice_at, first, count)
        for j, t in enumerate(blocks):
            source = buf.at[role, j, :, pl.ds(first, count)]
            if j == len(blocks) - 1 and chips[-1] == 0:
                c = pltpu.make_async_copy(source, out.at[:, where], local_sem.at[sem])
                c.start()
                kept.append(c)
            else:
                pltpu.make_async_remote_copy(
                    src_ref=source, dst_ref=out.at[:, where],
                    send_sem=out_send.at[sem], recv_sem=out_recv.at[sem], **at(t)
                ).start()

    far = list(range(half - 1, -1, -1))
    for role in range(2):
        targets(far, role, full, obuf, slice_for(role, b), shared, w - shared, role)
    for role in range(2):
        drain(outer_buf.at[role], outer_recv.at[role, 0], 1)
        drain(outer_buf.at[role], outer_recv.at[role, 1], nb - 2)
        for q in range(0, shared, step):
            columns = pl.ds(q, step)
            outer_full[role, :, columns] = (
                outer_buf[role, :, :, columns].astype(jnp.float32).reshape(total, step).astype(jnp.bfloat16)
            )
        targets(far[1:], role, outer_full, outer_obuf, outer_slice(role, b), 0, shared, 2 + role)
    for role in range(2):
        targets([0], role, full, obuf, slice_for(role, b), 0, shared, 4 + role)

    col_out[...] = column
    pot[...] = jnp.broadcast_to(row, (total, 128)).reshape(nb, rows, 128)
    diagonal = lax.broadcasted_iota(jnp.int32, (rows, 128), 0) == lax.broadcasted_iota(
        jnp.int32, (rows, 128), 1
    )
    flat = jnp.sum(jnp.where(diagonal, pot[b], 0.0), axis=0, keepdims=True)
    row_out[...] = flat[:, :rows]

    for role in range(2):
        for d in range(half):
            drain(data_buf.at[role], first_send.at[role, d], 2 if d else 1)
            drain(data_buf.at[role], on_send.at[role, d], 2)
        drain(noise_buf.at[role], noise_send.at[role], nb // 2 - 1)
    drain(norm_b, small_send.at[0], nf - 1)
    drain(a_buf, small_send.at[1], nf - 1)
    drain(b_buf, small_send.at[2], nb - 1)
    drain(c_buf, small_send.at[3], nf - 1)
    for role in range(2):
        drain(outer_buf.at[role], outer_send.at[role, 0], 1)
        drain(outer_buf.at[role], outer_send.at[role, 1], nb - 2)
        for sem, first, count, blocks in (
            (role, shared, w - shared, nb // 2 - 1), (2 + role, 0, shared, nb // 2 - 3), (4 + role, 0, shared, 1)
        ):
            view = obuf.at[role, pl.ds(0, blocks), :, pl.ds(first, count)]
            pltpu.make_async_copy(view, view, out_send.at[sem]).wait()
            pltpu.make_async_copy(view, view, out_recv.at[sem]).wait()
    for c in kept:
        c.wait()


def solution(mesh):
    nb, nf = mesh.shape["batch"], mesh.shape["feat"]

    def per_device(noise, data):
        rows, width = noise.shape
        total, w = rows * nb, width // nb
        piece, shared = total // nf, w * SHARED // 8
        targets, row, column = pl.pallas_call(
            functools.partial(kernel, nb, nf),
            out_shape=(
                jax.ShapeDtypeStruct((rows, width), jnp.bfloat16),
                jax.ShapeDtypeStruct((1, rows), jnp.float32),
                jax.ShapeDtypeStruct((1, total), jnp.float32),
            ),
            in_specs=[pl.BlockSpec(memory_space=pl.ANY)] * 2,
            out_specs=(
                pl.BlockSpec(memory_space=pl.ANY),
                pl.BlockSpec(memory_space=pltpu.VMEM),
                pl.BlockSpec(memory_space=pltpu.VMEM),
            ),
            scratch_shapes=[
                pltpu.VMEM((2, nb // 2, rows, w), jnp.bfloat16),
                pltpu.VMEM((2, nb, rows, w), jnp.bfloat16),
                pltpu.VMEM((2, nb, rows, shared), jnp.bfloat16),
                pltpu.VMEM((2, total, w), jnp.bfloat16),
                pltpu.VMEM((2, total, shared), jnp.bfloat16),
                pltpu.VMEM((2, rows, width), jnp.bfloat16),
                pltpu.VMEM((2, nb // 2, rows, w), jnp.bfloat16),
                pltpu.VMEM((2, nb // 2 - 2, rows, shared), jnp.bfloat16),
                pltpu.VMEM((nf, piece, total), jnp.float32),
                pltpu.VMEM((nf, piece, total), jnp.float32),
                pltpu.VMEM((piece + rows, total), jnp.float32),
                pltpu.VMEM((nb, piece + rows, total), jnp.float32),
                pltpu.VMEM((piece, total), jnp.float32),
                pltpu.VMEM((nf, piece, total), jnp.float32),
                pltpu.VMEM((rows, 128), jnp.float32),
                pltpu.VMEM((nf, rows, 128), jnp.float32),
                pltpu.VMEM((nb, rows, 128), jnp.float32),
                pltpu.VMEM((nb, rows, total), jnp.float32),
                pltpu.SemaphoreType.DMA((8,)),
                pltpu.SemaphoreType.DMA((2, 2)),
                pltpu.SemaphoreType.DMA((2, 2)),
                pltpu.SemaphoreType.DMA((2, nb // 4)),
                pltpu.SemaphoreType.DMA((2, nb // 4)),
                pltpu.SemaphoreType.DMA((2,)),
                pltpu.SemaphoreType.DMA((2,)),
                pltpu.SemaphoreType.DMA((2, nb // 4)),
                pltpu.SemaphoreType.DMA((2, nb // 4)),
                pltpu.SemaphoreType.DMA((4,)),
                pltpu.SemaphoreType.DMA((4,)),
                pltpu.SemaphoreType.DMA((6,)),
                pltpu.SemaphoreType.DMA((6,)),
            ],
            compiler_params=pltpu.CompilerParams(
                collective_id=0, has_side_effects=True, vmem_limit_bytes=56 * 2**20
            ),
        )(noise, data)
        return targets, row.reshape(rows), column.reshape(total)

    return jax.shard_map(
        per_device,
        mesh=mesh,
        in_specs=(P("batch", "feat"), P("batch", "feat")),
        out_specs=(P("batch", "feat"), P("batch"), P()),
        check_vma=False,
    )
```

```python
import functools
import math

import jax
import jax.numpy as jnp
from jax import lax
from jax.experimental import pallas as pl
from jax.experimental.pallas import tpu as pltpu
from jax.sharding import PartitionSpec as P

ITERS = 3
SHARED = 6
EARLY = 3
MESH = pl.DeviceIdType.MESH


def lse(values, axis):
    top = jnp.max(values, axis=axis, keepdims=True)
    return top + jnp.log(jnp.sum(jnp.exp(values - top), axis=axis, keepdims=True))


def far_first(count):
    return sorted(range(1, count), key=lambda k: (-min(k, count - k), k))


def kernel(
    nb, nf, noise, data, out, row_out, col_out,
    noise_buf, data_buf, outer_buf, full, outer_full, local_buf, obuf, outer_obuf, part, a_buf, own, b_buf, done, c_buf,
    norm_own, norm_own2, norm_b, pot, wbuf,
    local_sem, outer_send, outer_recv, first_send, first_recv, noise_send, noise_recv, on_send, on_recv,
    small_send, small_recv, out_send, out_recv,
):
    rows, width = noise.shape
    w = width // nb
    total = rows * nb
    features = width * nf
    root = math.sqrt(features)
    log_count = math.log(total)
    half = nb // 4
    shared = w * SHARED // 8
    b, f = lax.axis_index("batch"), lax.axis_index("feat")
    core = lax.rem(b, 2)
    sibling = b + 1 - 2 * core
    b_order, f_order = far_first(nb), list(range(1, nf))

    def at(t):
        return dict(device_id=(t, f), device_id_type=MESH)

    def in_column(k):
        return at(lax.rem(b + k, nb))

    def in_plane(k):
        return dict(device_id=(b, lax.rem(f + k, nf)), device_id_type=MESH)

    def drain(ref, sem, count):
        view = ref.at[pl.ds(0, count)]
        pltpu.make_async_copy(view, view, sem).wait()

    def wrap(t):
        return lax.rem(t + 2 * nb, nb)

    def columns_of(slice_at, q=0, n=w):
        return pl.ds(pl.multiple_of(slice_at * w + q, math.gcd(w, q)), n)

    def step_of(role):
        return 2 if role == 0 else -2

    barrier = pltpu.get_barrier_semaphore()
    for k in b_order:
        pl.semaphore_signal(barrier, inc=1, **in_column(k))
    for k in f_order:
        pl.semaphore_signal(barrier, inc=1, **in_plane(k))
    pl.semaphore_wait(barrier, nb + nf - 2)

    def slice_for(role, member):
        return wrap(member - 2 * role)

    for role in range(2):
        for member in (b, sibling):
            pltpu.make_async_remote_copy(
                src_ref=data.at[:, columns_of(slice_for(role, member))], dst_ref=data_buf.at[1 - role, b],
                send_sem=on_send.at[role, 0], recv_sem=on_recv.at[1 - role, 0],
                **at(wrap(member + step_of(role)))
            ).start()
    for d in range(half - 1, -1, -1):
        for role in range(2):
            for member in ([wrap(sibling + step_of(role) * d)] if d == 0 else []) + (
                [wrap(b + step_of(role) * d), wrap(sibling + step_of(role) * d)] if d else []
            ):
                pltpu.make_async_remote_copy(
                    src_ref=data.at[:, columns_of(slice_for(role, member))], dst_ref=data_buf.at[role, b],
                    send_sem=first_send.at[role, d], recv_sem=first_recv.at[role, d], **at(member)
                ).start()
    locals_ = []
    for role in range(2):
        s = columns_of(slice_for(role, b))
        locals_.append(pltpu.make_async_copy(data.at[:, s], data_buf.at[role, b], local_sem.at[role]))
        locals_.append(pltpu.make_async_copy(noise.at[:, s], noise_buf.at[role, core], local_sem.at[2 + role]))
    locals_.append(pltpu.make_async_copy(noise, local_buf.at[0], local_sem.at[4]))
    locals_.append(pltpu.make_async_copy(data, local_buf.at[1], local_sem.at[5]))
    def outer_slice(role, device):
        return slice_for(role, wrap(device + step_of(role)))

    for role in range(2):
        s = columns_of(outer_slice(role, b), 0, shared)
        locals_.append(pltpu.make_async_copy(data.at[:, s], outer_buf.at[role, b], local_sem.at[6 + role]))
    for c in locals_:
        c.start()
    for role in range(2):
        pltpu.make_async_remote_copy(
            src_ref=data.at[:, columns_of(outer_slice(role, sibling), 0, shared)],
            dst_ref=outer_buf.at[role, b],
            send_sem=outer_send.at[role, 0], recv_sem=outer_recv.at[role, 0], **at(sibling)
        ).start()
    for d in range(half - 1, -1, -1):
        for role in range(2):
            for member in [sibling] if d == 0 else [
                wrap(b + step_of(role) * d), wrap(sibling + step_of(role) * d)
            ]:
                pltpu.make_async_remote_copy(
                    src_ref=noise.at[:, columns_of(slice_for(role, member))],
                    dst_ref=noise_buf.at[role, 2 * d + core],
                    send_sem=noise_send.at[role], recv_sem=noise_recv.at[role], **at(member)
                ).start()
    for c in locals_:
        c.wait()

    def exchange(src_of, buf, slot, partner, order, sem):
        for k in order:
            pltpu.make_async_remote_copy(
                src_ref=src_of(k), dst_ref=buf.at[slot],
                send_sem=small_send.at[sem], recv_sem=small_recv.at[sem], **partner(k)
            ).start()

    chunk = min(2048, width)
    sums = []
    for i in range(2):
        def add(step, acc, i=i):
            v = local_buf[i, :, pl.ds(pl.multiple_of(step * chunk, chunk), chunk)].astype(jnp.float32)
            v = v * v
            for q in range(chunk // 128):
                acc = acc + v[:, q * 128:(q + 1) * 128]
            return acc
        acc = lax.fori_loop(0, width // chunk, add, jnp.zeros((rows, 128), jnp.float32))
        sums.append(jnp.sum(acc, axis=1, keepdims=True))
    lane = lax.broadcasted_iota(jnp.int32, (rows, 128), 1)
    norm_own[...] = jnp.where(lane < 64, sums[0], sums[1])
    norm_b[f] = norm_own[...]
    exchange(lambda k: norm_own, norm_b, f, in_plane, f_order, 0)

    def pair(chip_of):
        return pl.ds(pl.multiple_of(wrap(chip_of) // 2 * 2, 2), 2)

    for d in range(half - 1, 0, -1):
        for role in range(2):
            drain(data_buf.at[role], first_recv.at[role, d], 2)
            block = pair(b - step_of(role) * d)
            pltpu.make_async_remote_copy(
                src_ref=data_buf.at[role, block], dst_ref=data_buf.at[1 - role, block],
                send_sem=on_send.at[role, d], recv_sem=on_recv.at[1 - role, d],
                **at(wrap(b + step_of(role)))
            ).start()
    for role in range(2):
        drain(data_buf.at[role], first_recv.at[role, 0], 1)

    drain(norm_b, small_recv.at[0], nf - 1)
    norms = jnp.sum(norm_b[...], axis=0)
    diagonal = lax.broadcasted_iota(jnp.int32, (rows, 128), 0) == lane
    along = jnp.sum(jnp.where(diagonal, norms[:, 64:65], 0.0), axis=0, keepdims=True)
    along = pltpu.roll(jnp.broadcast_to(along, (rows, 128)), b * rows, 1)
    norm_own2[...] = -along - jnp.where(b == f, norms[:, :1], 0.0)

    for role in range(2):
        drain(noise_buf.at[role], noise_recv.at[role], nb // 2 - 1)
    for d in range(half):
        for role in range(2):
            drain(data_buf.at[role], on_recv.at[role, d], 2)

    def share(offsets):
        for d in offsets:
            for role in range(2):
                block = pair(b + step_of(role) * d)
                pltpu.make_async_remote_copy(
                    src_ref=data_buf.at[role, block, :, pl.ds(0, shared)], dst_ref=outer_buf.at[role, block],
                    send_sem=outer_send.at[role, 1], recv_sem=outer_recv.at[role, 1],
                    **at(wrap(b - step_of(role)))
                ).start()

    onward = list(range(nb // 2 - 1))
    share(onward[:EARLY])

    chunk = min(1024, w)
    served = total // 2
    for role in range(2):
        acc = jnp.zeros((served, total), jnp.float32)
        for q in range(w // chunk):
            columns = pl.ds(q * chunk, chunk)
            left = noise_buf[role, :, :, columns].astype(jnp.float32).reshape(served, chunk).astype(jnp.bfloat16)
            right = data_buf[role, :, :, columns].astype(jnp.float32).reshape(total, chunk).astype(jnp.bfloat16)
            acc = acc + lax.dot_general(
                left, right, (((1,), (1,)), ((), ())), preferred_element_type=jnp.float32
            )
        acc = acc.reshape(half, 2, rows, total)
        for d in range(half):
            block = pair(b - step_of(role) * d)
            if role and not d:
                part[block] = part[block] + acc[d]
            else:
                part[block] = acc[d]
    part[pair(b + nb // 2)] = jnp.zeros((2, rows, total), jnp.float32)

    a_buf[f] = part[f]
    exchange(lambda k: part.at[lax.rem(f + k, nf)], a_buf, f, in_plane, f_order, 1)
    drain(a_buf, small_recv.at[1], nf - 1)
    own[...] = 2.0 * jnp.sum(a_buf[...], axis=0) + norm_own2[...]
    b_buf[b] = own[...]
    exchange(lambda k: own, b_buf, b, in_column, b_order, 2)
    share(onward[EARLY:])
    for role in range(2):
        for q in range(w // chunk):
            columns = pl.ds(q * chunk, chunk)
            full[role, :, columns] = (
                data_buf[role, :, :, columns].astype(jnp.float32).reshape(total, chunk).astype(jnp.bfloat16)
            )
    drain(b_buf, small_recv.at[2], nb - 1)
    done[...] = jnp.sum(b_buf[...], axis=0)
    c_buf[f] = done[...]
    exchange(lambda k: done, c_buf, f, in_plane, f_order, 3)
    drain(c_buf, small_recv.at[3], nf - 1)
    scores = c_buf[...].reshape(total, total) / root + 2.0 * root
    column = jnp.zeros((1, total), jnp.float32)
    for _ in range(ITERS):
        row = -log_count - lse(scores + column, 1)
        column = -log_count - lse(scores + row, 0)
    plan = jnp.exp(scores + row + column)
    weights = plan / jnp.sum(plan, axis=1, keepdims=True)
    wbuf[...] = weights.reshape(nb, rows, total)

    step = math.gcd(512, shared)
    kept = []

    def targets(chips, role, values, buf, first, count):
        blocks = []
        for d in chips:
            blocks += [wrap(sibling - step_of(role) * d), wrap(b - step_of(role) * d)]
        chosen = jnp.concatenate([wbuf[t] for t in blocks], axis=0).astype(jnp.bfloat16)
        for q in range(0, count, step):
            n = min(step, count - q)
            summed = jnp.dot(chosen, values[role, :, first + q:first + q + n], preferred_element_type=jnp.float32)
            buf[role, :len(blocks), :, first + q:first + q + n] = summed.reshape(
                len(blocks), rows, n
            ).astype(jnp.bfloat16)

    def to_device(source, where, t, sem):
        pltpu.make_async_remote_copy(
            src_ref=source, dst_ref=out.at[:, where],
            send_sem=out_send.at[sem], recv_sem=out_recv.at[sem], **at(t)
        ).start()

    def to_own(buf, role, place, slice_at, first, count, sem):
        where = columns_of(slice_at, first, count)
        to_device(buf.at[role, place, :, pl.ds(first, count)], where, sibling, sem)
        c = pltpu.make_async_copy(
            buf.at[role, place + 1, :, pl.ds(first, count)], out.at[:, where], local_sem.at[sem]
        )
        c.start()
        kept.append(c)

    def to_chips(chips, buf, slice_of, first, count, sem, wanted):
        for q in wanted:
            for role in range(2):
                d = lax.rem((b // 2 - q if role == 0 else q - b // 2) + nb, nb // 2)

                @pl.when((d >= max(chips[-1], 1)) & (d <= chips[0]))
                def _(q=q, role=role, d=d):
                    where = columns_of(slice_of(role, b), first, count)
                    for i, t in enumerate((2 * q + 1 - core, 2 * q + core)):
                        place = 2 * (chips[0] - d) + i
                        to_device(buf.at[role, place, :, pl.ds(first, count)], where, t, sem + role)

    far = list(range(half - 1, -1, -1))
    low, high = range(nb // 4), range(nb // 4, nb // 2)
    inner = (far, obuf, slice_for, shared, w - shared, 0)
    outer = (far[1:], outer_obuf, outer_slice, 0, shared, 2)
    for role in range(2):
        targets(far, role, full, obuf, shared, w - shared)
    to_chips(*inner, low)
    to_chips(*inner, high)
    for role in range(2):
        to_own(obuf, role, nb // 2 - 2, slice_for(role, b), shared, w - shared, role)
    for role in range(2):
        drain(outer_buf.at[role], outer_recv.at[role, 0], 1)
        drain(outer_buf.at[role], outer_recv.at[role, 1], nb - 2)
        for q in range(0, shared, step):
            columns = pl.ds(q, step)
            outer_full[role, :, columns] = (
                outer_buf[role, :, :, columns].astype(jnp.float32).reshape(total, step).astype(jnp.bfloat16)
            )
        targets(far[1:], role, outer_full, outer_obuf, 0, shared)
    to_chips(*outer, low)
    for role in range(2):
        to_own(outer_obuf, role, nb // 2 - 4, outer_slice(role, b), 0, shared, 2 + role)
    for role in range(2):
        targets([0], role, full, obuf, 0, shared)
        to_own(obuf, role, 0, slice_for(role, b), 0, shared, 4 + role)
    to_chips(*outer, high)

    col_out[...] = column
    pot[...] = jnp.broadcast_to(row, (total, 128)).reshape(nb, rows, 128)
    flat = jnp.sum(jnp.where(diagonal, pot[b], 0.0), axis=0, keepdims=True)
    row_out[...] = flat[:, :rows]

    for role in range(2):
        for d in range(half):
            drain(data_buf.at[role], first_send.at[role, d], 2 if d else 1)
            drain(data_buf.at[role], on_send.at[role, d], 2)
        drain(noise_buf.at[role], noise_send.at[role], nb // 2 - 1)
    drain(norm_b, small_send.at[0], nf - 1)
    drain(a_buf, small_send.at[1], nf - 1)
    drain(b_buf, small_send.at[2], nb - 1)
    drain(c_buf, small_send.at[3], nf - 1)
    for role in range(2):
        drain(outer_buf.at[role], outer_send.at[role, 0], 1)
        drain(outer_buf.at[role], outer_send.at[role, 1], nb - 2)
        for sem, first, count, blocks in (
            (role, shared, w - shared, nb // 2 - 1), (2 + role, 0, shared, nb // 2 - 3), (4 + role, 0, shared, 1)
        ):
            view = obuf.at[role, pl.ds(0, blocks), :, pl.ds(first, count)]
            pltpu.make_async_copy(view, view, out_send.at[sem]).wait()
            pltpu.make_async_copy(view, view, out_recv.at[sem]).wait()
    for c in kept:
        c.wait()


def solution(mesh):
    nb, nf = mesh.shape["batch"], mesh.shape["feat"]

    def per_device(noise, data):
        rows, width = noise.shape
        total, w = rows * nb, width // nb
        piece, shared = total // nf, w * SHARED // 8
        targets, row, column = pl.pallas_call(
            functools.partial(kernel, nb, nf),
            out_shape=(
                jax.ShapeDtypeStruct((rows, width), jnp.bfloat16),
                jax.ShapeDtypeStruct((1, rows), jnp.float32),
                jax.ShapeDtypeStruct((1, total), jnp.float32),
            ),
            in_specs=[pl.BlockSpec(memory_space=pl.ANY)] * 2,
            out_specs=(
                pl.BlockSpec(memory_space=pltpu.VMEM),
                pl.BlockSpec(memory_space=pltpu.VMEM),
                pl.BlockSpec(memory_space=pltpu.VMEM),
            ),
            scratch_shapes=[
                pltpu.VMEM((2, nb // 2, rows, w), jnp.bfloat16),
                pltpu.VMEM((2, nb, rows, w), jnp.bfloat16),
                pltpu.VMEM((2, nb, rows, shared), jnp.bfloat16),
                pltpu.VMEM((2, total, w), jnp.bfloat16),
                pltpu.VMEM((2, total, shared), jnp.bfloat16),
                pltpu.VMEM((2, rows, width), jnp.bfloat16),
                pltpu.VMEM((2, nb // 2, rows, w), jnp.bfloat16),
                pltpu.VMEM((2, nb // 2 - 2, rows, shared), jnp.bfloat16),
                pltpu.VMEM((nf, piece, total), jnp.float32),
                pltpu.VMEM((nf, piece, total), jnp.float32),
                pltpu.VMEM((piece, total), jnp.float32),
                pltpu.VMEM((nb, piece, total), jnp.float32),
                pltpu.VMEM((piece, total), jnp.float32),
                pltpu.VMEM((nf, piece, total), jnp.float32),
                pltpu.VMEM((rows, 128), jnp.float32),
                pltpu.VMEM((rows, 128), jnp.float32),
                pltpu.VMEM((nf, rows, 128), jnp.float32),
                pltpu.VMEM((nb, rows, 128), jnp.float32),
                pltpu.VMEM((nb, rows, total), jnp.float32),
                pltpu.SemaphoreType.DMA((8,)),
                pltpu.SemaphoreType.DMA((2, 2)),
                pltpu.SemaphoreType.DMA((2, 2)),
                pltpu.SemaphoreType.DMA((2, nb // 4)),
                pltpu.SemaphoreType.DMA((2, nb // 4)),
                pltpu.SemaphoreType.DMA((2,)),
                pltpu.SemaphoreType.DMA((2,)),
                pltpu.SemaphoreType.DMA((2, nb // 4)),
                pltpu.SemaphoreType.DMA((2, nb // 4)),
                pltpu.SemaphoreType.DMA((4,)),
                pltpu.SemaphoreType.DMA((4,)),
                pltpu.SemaphoreType.DMA((6,)),
                pltpu.SemaphoreType.DMA((6,)),
            ],
            compiler_params=pltpu.CompilerParams(
                collective_id=0, has_side_effects=True, vmem_limit_bytes=52 * 2**20
            ),
        )(noise, data)
        return targets, row.reshape(rows), column.reshape(total)

    return jax.shard_map(
        per_device,
        mesh=mesh,
        in_specs=(P("batch", "feat"), P("batch", "feat")),
        out_specs=(P("batch", "feat"), P("batch"), P()),
        check_vma=False,
    )
```

```python
import functools
import math

import jax
import jax.numpy as jnp
from jax import lax
from jax.experimental import pallas as pl
from jax.experimental.pallas import tpu as pltpu
from jax.sharding import PartitionSpec as P

ITERS = 3
SHARED = 7
EARLY = 3
MESH = pl.DeviceIdType.MESH


def lse(values, axis):
    top = jnp.max(values, axis=axis, keepdims=True)
    return top + jnp.log(jnp.sum(jnp.exp(values - top), axis=axis, keepdims=True))


def far_first(count):
    return sorted(range(1, count), key=lambda k: (-min(k, count - k), k))


def kernel(
    nb, nf, noise, data, out, row_out, col_out,
    noise_buf, data_buf, outer_buf, full, outer_full, local_buf, obuf, outer_obuf,
    part, a_buf, own, b_buf, done, c_buf, norm_own, norm_b, pot, wbuf,
    local_sem, outer_send, outer_recv, first_send, first_recv, noise_send, noise_recv, on_send, on_recv,
    small_send, small_recv, out_send, out_recv,
):
    rows, width = noise.shape
    w = width // nb
    total = rows * nb
    piece = total // nf
    features = width * nf
    root = math.sqrt(features)
    log_count = math.log(total)
    half = nb // 4
    shared = w * SHARED // 8
    b, f = lax.axis_index("batch"), lax.axis_index("feat")
    core = lax.rem(b, 2)
    sibling = b + 1 - 2 * core
    b_order, f_order = far_first(nb), list(range(1, nf))

    def at(t):
        return dict(device_id=(t, f), device_id_type=MESH)

    def in_column(k):
        return at(lax.rem(b + k, nb))

    def in_plane(k):
        return dict(device_id=(b, lax.rem(f + k, nf)), device_id_type=MESH)

    def drain(ref, sem, count):
        view = ref.at[pl.ds(0, count)]
        pltpu.make_async_copy(view, view, sem).wait()

    def wrap(t):
        return lax.rem(t + 2 * nb, nb)

    def pair(device):
        return pl.ds(pl.multiple_of(wrap(device) // 2 * 2, 2), 2)

    def columns_of(slice_at, q=0, n=w):
        return pl.ds(pl.multiple_of(slice_at * w + q, math.gcd(w, q)), n)

    def step_of(role):
        return 2 if role == 0 else -2

    def slice_for(role, member):
        return wrap(member - 2 * role)

    def outer_slice(role, device):
        return slice_for(role, wrap(device + step_of(role)))

    def remote(source, target, send, recv, device):
        pltpu.make_async_remote_copy(
            src_ref=source, dst_ref=target, send_sem=send, recv_sem=recv, **device
        ).start()

    barrier = pltpu.get_barrier_semaphore()
    for k in b_order:
        pl.semaphore_signal(barrier, inc=1, **in_column(k))
    for k in f_order:
        pl.semaphore_signal(barrier, inc=1, **in_plane(k))
    pl.semaphore_wait(barrier, nb + nf - 2)

    for role in range(2):
        for member in (b, sibling):
            remote(
                data.at[:, columns_of(slice_for(role, member))], data_buf.at[1 - role, b],
                on_send.at[role, 0], on_recv.at[1 - role, 0], at(wrap(member + step_of(role))),
            )
    for d in range(half - 1, -1, -1):
        for role in range(2):
            for member in [sibling] if d == 0 else [
                wrap(b + step_of(role) * d), wrap(sibling + step_of(role) * d)
            ]:
                source = data.at[:, columns_of(slice_for(role, member))]
                if d > 1:
                    remote(
                        source, outer_buf.at[role, b],
                        first_send.at[role, d], outer_recv.at[role, d], at(wrap(member - step_of(role))),
                    )
                else:
                    remote(
                        source, data_buf.at[role, b], first_send.at[role, d], first_recv.at[role, d], at(member)
                    )
    locals_ = []
    for role in range(2):
        s = columns_of(slice_for(role, b))
        locals_.append(pltpu.make_async_copy(data.at[:, s], data_buf.at[role, b], local_sem.at[role]))
        locals_.append(pltpu.make_async_copy(noise.at[:, s], noise_buf.at[role, core], local_sem.at[2 + role]))
        s = columns_of(outer_slice(role, b))
        locals_.append(pltpu.make_async_copy(data.at[:, s], outer_buf.at[role, b], local_sem.at[6 + role]))
    locals_.append(pltpu.make_async_copy(noise, local_buf.at[0], local_sem.at[4]))
    locals_.append(pltpu.make_async_copy(data, local_buf.at[1], local_sem.at[5]))
    for c in locals_:
        c.start()
    for role in range(2):
        remote(
            data.at[:, columns_of(outer_slice(role, sibling))], outer_buf.at[role, b],
            outer_send.at[role, 0], outer_recv.at[role, 0], at(sibling),
        )

    def send_noise(distances):
        for d in distances:
            for role in range(2):
                for member in [sibling] if d == 0 else [
                    wrap(b + step_of(role) * d), wrap(sibling + step_of(role) * d)
                ]:
                    remote(
                        noise.at[:, columns_of(slice_for(role, member))], noise_buf.at[role, 2 * d + core],
                        noise_send.at[role], noise_recv.at[role], at(member),
                    )

    send_noise([half - 1])
    for c in locals_:
        c.wait()

    def exchange(src_of, buf, slot, partner, order, sem):
        for k in order:
            remote(src_of(k), buf.at[slot], small_send.at[sem], small_recv.at[sem], partner(k))

    chunk = min(2048, width)
    sums = []
    for i in range(2):
        def add(step, acc, i=i):
            v = local_buf[i, :, pl.ds(pl.multiple_of(step * chunk, chunk), chunk)].astype(jnp.float32)
            v = v * v
            for q in range(chunk // 128):
                acc = acc + v[:, q * 128:(q + 1) * 128]
            return acc
        acc = lax.fori_loop(0, width // chunk, add, jnp.zeros((rows, 128), jnp.float32))
        sums.append(jnp.sum(acc, axis=1, keepdims=True))
    lane = lax.broadcasted_iota(jnp.int32, (rows, 128), 1)
    sublane = lax.broadcasted_iota(jnp.int32, (rows, 128), 0)
    norm_own[...] = jnp.where(lane < 64, sums[0], sums[1])
    norm_b[f] = norm_own[...]
    exchange(lambda k: norm_own, norm_b, f, in_plane, f_order, 0)

    def onward(d):
        for role in range(2):
            drain(data_buf.at[role], first_recv.at[role, d], 2)
            block = pair(b - step_of(role) * d)
            remote(
                data_buf.at[role, block], data_buf.at[1 - role, block],
                on_send.at[role, d], on_recv.at[1 - role, d], at(wrap(b + step_of(role))),
            )

    for d in range(half - 1, 1, -1):
        for role in range(2):
            drain(outer_buf.at[role], outer_recv.at[role, d], 2)
            block = pair(b - step_of(role) * (d - 1))
            remote(
                outer_buf.at[role, block], data_buf.at[role, block],
                outer_send.at[role, d], first_recv.at[role, d], at(wrap(b + step_of(role))),
            )
    onward(1)
    send_noise(range(half - 2, 1, -1))
    for d in range(half - 1, 1, -1):
        onward(d)
    send_noise([1, 0])

    drain(norm_b, small_recv.at[0], nf - 1)
    norms = jnp.sum(norm_b[...], axis=0)
    picked = jnp.where(lane == sublane, norms[:, :1], jnp.where(lane == sublane + rows, norms[:, 64:65], 0.0))
    own[piece:, :] = jnp.sum(picked, axis=0, keepdims=True)

    for role in range(2):
        drain(data_buf.at[role], first_recv.at[role, 0], 1)
        for d in range(half):
            drain(data_buf.at[role], on_recv.at[role, d], 2)
    def share(offsets):
        for d in offsets:
            for role in range(2):
                block = pair(b + step_of(role) * d)
                remote(
                    data_buf.at[role, block, :, pl.ds(0, shared)], outer_buf.at[role, block, :, pl.ds(0, shared)],
                    outer_send.at[role, 1], outer_recv.at[role, 1], at(wrap(b - step_of(role))),
                )

    offsets = list(range(half + 1))
    share(offsets[:EARLY])

    chunk = min(1024, w)
    for role in range(2):
        for q in range(w // chunk):
            columns = pl.ds(q * chunk, chunk)
            full[role, :, columns] = (
                data_buf[role, :, :, columns].astype(jnp.float32).reshape(total, chunk).astype(jnp.bfloat16)
            )
    for role in range(2):
        drain(noise_buf.at[role], noise_recv.at[role], nb // 2 - 1)

    served = total // 2
    for role in range(2):
        acc = jnp.zeros((served, total), jnp.float32)
        for q in range(w // chunk):
            columns = pl.ds(q * chunk, chunk)
            left = noise_buf[role, :, :, columns].astype(jnp.float32).reshape(served, chunk).astype(jnp.bfloat16)
            acc = acc + lax.dot_general(
                left, full[role, :, columns], (((1,), (1,)), ((), ())), preferred_element_type=jnp.float32
            )
        acc = acc.reshape(half, 2, rows, total)
        for d in range(half):
            block = pair(b - step_of(role) * d)
            if role and not d:
                part[block] = part[block] + acc[d]
            else:
                part[block] = acc[d]
    part[pair(b + nb // 2)] = jnp.zeros((2, rows, total), jnp.float32)

    part_of = part.reshape(nf, piece, total) if piece != rows else part
    a_buf[f] = part_of[f]
    exchange(lambda k: part_of.at[lax.rem(f + k, nf)], a_buf, f, in_plane, f_order, 1)
    drain(a_buf, small_recv.at[1], nf - 1)
    own[:piece, :] = jnp.sum(a_buf[...], axis=0)
    b_buf[b] = own[...]
    exchange(lambda k: own, b_buf, b, in_column, b_order, 2)
    share(offsets[EARLY:])
    drain(b_buf, small_recv.at[2], nb - 1)
    done[...] = jnp.sum(b_buf[:, :piece, :], axis=0)
    c_buf[f] = done[...]
    exchange(lambda k: done, c_buf, f, in_plane, f_order, 3)
    norms = jnp.broadcast_to(b_buf[:, piece:, :], (nb, rows, 128))
    noise_norm = jnp.sum(jnp.where(lane == sublane, norms, 0.0), axis=2, keepdims=True).reshape(total, 1)
    data_norm = jnp.sum(jnp.where(lane == sublane + rows, norms, 0.0), axis=2, keepdims=True).reshape(total, 1)
    data_norm = jnp.transpose(jnp.broadcast_to(data_norm, (total, 128)))[:1, :]
    drain(c_buf, small_recv.at[3], nf - 1)
    cross = c_buf[...].reshape(total, total)

    scores = (2.0 * cross - noise_norm - data_norm) / root + 2.0 * root
    column = jnp.zeros((1, total), jnp.float32)
    for _ in range(ITERS):
        row = -log_count - lse(scores + column, 1)
        column = -log_count - lse(scores + row, 0)
    plan = jnp.exp(scores + row + column)
    weights = plan / jnp.sum(plan, axis=1, keepdims=True)
    wbuf[...] = weights.reshape(nb, rows, total)

    parts = 2
    step = math.gcd(512, shared // parts)
    kept = []

    def targets(chips, role, values, buf, first, count):
        blocks = []
        for d in chips:
            blocks += [wrap(sibling - step_of(role) * d), wrap(b - step_of(role) * d)]
        chosen = jnp.concatenate([wbuf[t] for t in blocks], axis=0).astype(jnp.bfloat16)
        for q in range(first, first + count, step):
            summed = jnp.dot(chosen, values[role, :, q:q + step], preferred_element_type=jnp.float32)
            buf[role, :len(blocks), :, q:q + step] = summed.reshape(len(blocks), rows, step).astype(jnp.bfloat16)

    def to_own(buf, role, place, slice_at, first, count, sem):
        where = columns_of(slice_at, first, count)
        remote(
            buf.at[role, place, :, pl.ds(first, count)], out.at[:, where],
            out_send.at[sem], out_recv.at[sem], at(sibling),
        )
        c = pltpu.make_async_copy(
            buf.at[role, place + 1, :, pl.ds(first, count)], out.at[:, where], local_sem.at[sem]
        )
        c.start()
        kept.append(c)

    def to_chips(chips, buf, slice_of, first, count, sem, roles):
        for q in range(nb // 2):
            for role in roles:
                d = lax.rem((b // 2 - q if role == 0 else q - b // 2) + nb, nb // 2)

                @pl.when((d >= max(chips[-1], 1)) & (d <= chips[0]))
                def _(q=q, role=role, d=d):
                    where = columns_of(slice_of(role, b), first, count)
                    for i, t in enumerate((2 * q + 1 - core, 2 * q + core)):
                        place = 2 * (chips[0] - d) + i
                        remote(
                            buf.at[role, place, :, pl.ds(first, count)], out.at[:, where],
                            out_send.at[sem + role], out_recv.at[sem + role], at(t),
                        )

    far = list(range(half - 1, -1, -1))
    groups = []
    if shared < w:
        for role in range(2):
            targets(far, role, full, obuf, shared, w - shared)
        to_chips(far, obuf, slice_for, shared, w - shared, 0, (0, 1))
        for role in range(2):
            to_own(obuf, role, nb // 2 - 2, slice_for(role, b), shared, w - shared, role)
            groups.append((role, shared, w - shared, nb // 2 - 1))
    for role in range(2):
        targets([0], role, full, obuf, 0, shared)
        to_own(obuf, role, 0, slice_for(role, b), 0, shared, 2 + role)
        groups.append((2 + role, 0, shared, 1))
    for role in range(2):
        drain(outer_buf.at[role], outer_recv.at[role, 0], 1)
        view = outer_buf.at[role, pl.ds(0, 2 * len(offsets)), :, pl.ds(0, shared)]
        pltpu.make_async_copy(view, view, outer_recv.at[role, 1]).wait()
    n = shared // parts
    for g in range(parts):
        for role in range(2):
            for q in range(g * n, (g + 1) * n, step):
                columns = pl.ds(q, step)
                outer_full[role, :, columns] = (
                    outer_buf[role, :, :, columns].astype(jnp.float32).reshape(total, step).astype(jnp.bfloat16)
                )
            targets(far[1:], role, outer_full, outer_obuf, g * n, n)
        sem = 4 + 2 * g
        to_chips(far[1:], outer_obuf, outer_slice, g * n, n, sem, (0, 1))
        for role in range(2):
            to_own(outer_obuf, role, nb // 2 - 4, outer_slice(role, b), g * n, n, sem + role)
            groups.append((sem + role, g * n, n, nb // 2 - 3))

    col_out[...] = column
    pot[...] = jnp.broadcast_to(row, (total, 128)).reshape(nb, rows, 128)
    row_out[...] = jnp.sum(jnp.where(lane == sublane, pot[b], 0.0), axis=0, keepdims=True)[:, :rows]

    for role in range(2):
        for d in range(half):
            drain(data_buf.at[role], first_send.at[role, d], 2 if d else 1)
            drain(data_buf.at[role], on_send.at[role, d], 2)
        for d in range(half - 1, 1, -1):
            drain(data_buf.at[role], outer_send.at[role, d], 2)
        drain(outer_buf.at[role], outer_send.at[role, 0], 1)
        view = outer_buf.at[role, pl.ds(0, 2 * len(offsets)), :, pl.ds(0, shared)]
        pltpu.make_async_copy(view, view, outer_send.at[role, 1]).wait()
        drain(noise_buf.at[role], noise_send.at[role], nb // 2 - 1)
    drain(norm_b, small_send.at[0], nf - 1)
    drain(a_buf, small_send.at[1], nf - 1)
    drain(b_buf, small_send.at[2], nb - 1)
    drain(c_buf, small_send.at[3], nf - 1)
    for sem, first, count, blocks in groups:
        view = obuf.at[0, pl.ds(0, blocks), :, pl.ds(first, count)]
        pltpu.make_async_copy(view, view, out_send.at[sem]).wait()
        pltpu.make_async_copy(view, view, out_recv.at[sem]).wait()
    for c in kept:
        c.wait()


def solution(mesh):
    nb, nf = mesh.shape["batch"], mesh.shape["feat"]

    def per_device(noise, data):
        rows, width = noise.shape
        total, w = rows * nb, width // nb
        piece = total // nf
        targets, row, column = pl.pallas_call(
            functools.partial(kernel, nb, nf),
            out_shape=(
                jax.ShapeDtypeStruct((rows, width), jnp.bfloat16),
                jax.ShapeDtypeStruct((1, rows), jnp.float32),
                jax.ShapeDtypeStruct((1, total), jnp.float32),
            ),
            in_specs=[pl.BlockSpec(memory_space=pl.ANY)] * 2,
            out_specs=[pl.BlockSpec(memory_space=pltpu.VMEM)] * 3,
            scratch_shapes=[
                pltpu.VMEM((2, nb // 2, rows, w), jnp.bfloat16),
                pltpu.VMEM((2, nb, rows, w), jnp.bfloat16),
                pltpu.VMEM((2, nb, rows, w), jnp.bfloat16),
                pltpu.VMEM((2, total, w), jnp.bfloat16),
                pltpu.VMEM((2, total, w), jnp.bfloat16),
                pltpu.VMEM((2, rows, width), jnp.bfloat16),
                pltpu.VMEM((2, nb // 2, rows, w), jnp.bfloat16),
                pltpu.VMEM((2, nb // 2 - 2, rows, w), jnp.bfloat16),
                pltpu.VMEM((nb, rows, total), jnp.float32),
                pltpu.VMEM((nf, piece, total), jnp.float32),
                pltpu.VMEM((piece + 1, total), jnp.float32),
                pltpu.VMEM((nb, piece + 1, total), jnp.float32),
                pltpu.VMEM((piece, total), jnp.float32),
                pltpu.VMEM((nf, piece, total), jnp.float32),
                pltpu.VMEM((rows, 128), jnp.float32),
                pltpu.VMEM((nf, rows, 128), jnp.float32),
                pltpu.VMEM((nb, rows, 128), jnp.float32),
                pltpu.VMEM((nb, rows, total), jnp.float32),
                pltpu.SemaphoreType.DMA((8,)),
                pltpu.SemaphoreType.DMA((2, nb // 4)),
                pltpu.SemaphoreType.DMA((2, nb // 4)),
                pltpu.SemaphoreType.DMA((2, nb // 4)),
                pltpu.SemaphoreType.DMA((2, nb // 4)),
                pltpu.SemaphoreType.DMA((2,)),
                pltpu.SemaphoreType.DMA((2,)),
                pltpu.SemaphoreType.DMA((2, nb // 4)),
                pltpu.SemaphoreType.DMA((2, nb // 4)),
                pltpu.SemaphoreType.DMA((4,)),
                pltpu.SemaphoreType.DMA((4,)),
                pltpu.SemaphoreType.DMA((8,)),
                pltpu.SemaphoreType.DMA((8,)),
            ],
            compiler_params=pltpu.CompilerParams(
                collective_id=0, has_side_effects=True, vmem_limit_bytes=52 * 2**20
            ),
        )(noise, data)
        return targets, row.reshape(rows), column.reshape(total)

    return jax.shard_map(
        per_device,
        mesh=mesh,
        in_specs=(P("batch", "feat"), P("batch", "feat")),
        out_specs=(P("batch", "feat"), P("batch"), P()),
        check_vma=False,
    )
```

```python
import functools
import math

import jax
import jax.numpy as jnp
from jax import lax
from jax.experimental import pallas as pl
from jax.experimental.pallas import tpu as pltpu
from jax.sharding import PartitionSpec as P

ITERS = 3
SHARED = 7
EARLY = 3
MESH = pl.DeviceIdType.MESH


def lse(values, axis):
    top = jnp.max(values, axis=axis, keepdims=True)
    return top + jnp.log(jnp.sum(jnp.exp(values - top), axis=axis, keepdims=True))


def far_first(count):
    return sorted(range(1, count), key=lambda k: (-min(k, count - k), k))


def kernel(
    nb, nf, noise, data, out, row_out, col_out,
    noise_buf, data_buf, outer_buf, full, outer_full, local_buf, obuf, outer_obuf,
    part, a_buf, own, b_buf, done, c_buf, norm_own, norm_b, pot, wbuf,
    local_sem, outer_send, outer_recv, first_send, first_recv, noise_send, noise_recv, on_send, on_recv,
    small_send, small_recv, out_send, out_recv, arrived,
):
    rows, width = noise.shape
    w = width // nb
    total = rows * nb
    piece = total // nf
    features = width * nf
    root = math.sqrt(features)
    log_count = math.log(total)
    half = nb // 4
    shared = w * SHARED // 8
    b, f = lax.axis_index("batch"), lax.axis_index("feat")
    core = lax.rem(b, 2)
    sibling = b + 1 - 2 * core
    b_order, f_order = far_first(nb), list(range(1, nf))

    def at(t):
        return dict(device_id=(t, f), device_id_type=MESH)

    def in_column(k):
        return at(lax.rem(b + k, nb))

    def in_plane(k):
        return dict(device_id=(b, lax.rem(f + k, nf)), device_id_type=MESH)

    def drain(ref, sem, count):
        view = ref.at[pl.ds(0, count)]
        pltpu.make_async_copy(view, view, sem).wait()

    def wrap(t):
        return lax.rem(t + 2 * nb, nb)

    def pair(device):
        return pl.ds(pl.multiple_of(wrap(device) // 2 * 2, 2), 2)

    def columns_of(slice_at, q=0, n=w):
        return pl.ds(pl.multiple_of(slice_at * w + q, math.gcd(w, q)), n)

    def step_of(role):
        return 2 if role == 0 else -2

    def slice_for(role, member):
        return wrap(member - 2 * role)

    def outer_slice(role, device):
        return slice_for(role, wrap(device + step_of(role)))

    def remote(source, target, send, recv, device):
        pltpu.make_async_remote_copy(
            src_ref=source, dst_ref=target, send_sem=send, recv_sem=recv, **device
        ).start()

    side = math.isqrt(nf)
    fy, fx = f // side, lax.rem(f, side)

    def in_grid(y, x):
        place = lax.rem(fy + y + side, side) * side + lax.rem(fx + x + side, side)
        return dict(device_id=(b, place), device_id_type=MESH)

    beside = [in_column(2), in_column(nb - 2)]
    diagonal = [at(wrap(sibling + 2)), at(wrap(sibling - 2))]
    row_beside = [in_grid(0, 1), in_grid(0, -1)]
    column_beside = [in_grid(1, 0), in_grid(-1, 0)]
    barrier = pltpu.get_barrier_semaphore()
    near = beside + diagonal + [at(sibling)] + row_beside + column_beside
    for device in near:
        pl.semaphore_signal(barrier, inc=1, **device)
    pl.semaphore_wait(barrier, len(near))

    def tell(devices, which):
        for device in devices:
            pl.semaphore_signal(arrived.at[which], inc=1, **device)

    tell(beside, 0)
    tell(row_beside, 3)

    for role in range(2):
        for member in (b, sibling):
            remote(
                data.at[:, columns_of(slice_for(role, member))], data_buf.at[1 - role, b],
                on_send.at[role, 0], on_recv.at[1 - role, 0], at(wrap(member + step_of(role))),
            )
    def send_data(d):
        for role in range(2):
            for member in [sibling] if d == 0 else [
                wrap(b + step_of(role) * d), wrap(sibling + step_of(role) * d)
            ]:
                source = data.at[:, columns_of(slice_for(role, member))]
                if d > 1:
                    remote(
                        source, outer_buf.at[role, b],
                        first_send.at[role, d], outer_recv.at[role, d], at(wrap(member - step_of(role))),
                    )
                else:
                    remote(
                        source, data_buf.at[role, b], first_send.at[role, d], first_recv.at[role, d], at(member)
                    )
    send_data(2)
    pl.semaphore_wait(arrived.at[0], 2)
    tell(beside, 1)
    for d in (3, 1, 0):
        send_data(d)
    locals_ = []
    for role in range(2):
        s = columns_of(slice_for(role, b))
        locals_.append(pltpu.make_async_copy(data.at[:, s], data_buf.at[role, b], local_sem.at[role]))
        locals_.append(pltpu.make_async_copy(noise.at[:, s], noise_buf.at[role, core], local_sem.at[2 + role]))
        s = columns_of(outer_slice(role, b))
        locals_.append(pltpu.make_async_copy(data.at[:, s], outer_buf.at[role, b], local_sem.at[6 + role]))
    locals_.append(pltpu.make_async_copy(noise, local_buf.at[0], local_sem.at[4]))
    locals_.append(pltpu.make_async_copy(data, local_buf.at[1], local_sem.at[5]))
    for c in locals_:
        c.start()
    for role in range(2):
        remote(
            data.at[:, columns_of(outer_slice(role, sibling))], outer_buf.at[role, b],
            outer_send.at[role, 0], outer_recv.at[role, 0], at(sibling),
        )

    def send_noise(distances):
        for d in distances:
            for role in range(2):
                for member in [sibling] if d == 0 else [
                    wrap(b + step_of(role) * d), wrap(sibling + step_of(role) * d)
                ]:
                    remote(
                        noise.at[:, columns_of(slice_for(role, member))], noise_buf.at[role, 2 * d + core],
                        noise_send.at[role], noise_recv.at[role], at(member),
                    )

    pl.semaphore_wait(arrived.at[3], 2)
    tell(column_beside, 4)
    pl.semaphore_wait(arrived.at[1], 2)
    tell(beside, 2)
    send_noise([half - 1])
    pl.semaphore_wait(arrived.at[4], 2)
    tell(column_beside, 5)
    pl.semaphore_wait(arrived.at[2], 2)
    pl.semaphore_wait(arrived.at[5], 2)
    for c in locals_:
        c.wait()

    def exchange(src_of, buf, slot, partner, order, sem):
        for k in order:
            remote(src_of(k), buf.at[slot], small_send.at[sem], small_recv.at[sem], partner(k))

    chunk = min(2048, width)
    sums = []
    for i in range(2):
        def add(step, acc, i=i):
            v = local_buf[i, :, pl.ds(pl.multiple_of(step * chunk, chunk), chunk)].astype(jnp.float32)
            v = v * v
            for q in range(chunk // 128):
                acc = acc + v[:, q * 128:(q + 1) * 128]
            return acc
        acc = lax.fori_loop(0, width // chunk, add, jnp.zeros((rows, 128), jnp.float32))
        sums.append(jnp.sum(acc, axis=1, keepdims=True))
    lane = lax.broadcasted_iota(jnp.int32, (rows, 128), 1)
    sublane = lax.broadcasted_iota(jnp.int32, (rows, 128), 0)
    norm_own[...] = jnp.where(lane < 64, sums[0], sums[1])
    norm_b[f] = norm_own[...]
    exchange(lambda k: norm_own, norm_b, f, in_plane, f_order, 0)

    def onward(d):
        for role in range(2):
            drain(data_buf.at[role], first_recv.at[role, d], 2)
            block = pair(b - step_of(role) * d)
            remote(
                data_buf.at[role, block], data_buf.at[1 - role, block],
                on_send.at[role, d], on_recv.at[1 - role, d], at(wrap(b + step_of(role))),
            )

    for d in range(half - 1, 1, -1):
        for role in range(2):
            drain(outer_buf.at[role], outer_recv.at[role, d], 2)
            block = pair(b - step_of(role) * (d - 1))
            remote(
                outer_buf.at[role, block], data_buf.at[role, block],
                outer_send.at[role, d], first_recv.at[role, d], at(wrap(b + step_of(role))),
            )
    onward(1)
    send_noise(range(half - 2, 1, -1))
    for d in range(half - 1, 1, -1):
        onward(d)
    send_noise([1, 0])

    drain(norm_b, small_recv.at[0], nf - 1)
    norms = jnp.sum(norm_b[...], axis=0)
    picked = jnp.where(lane == sublane, norms[:, :1], jnp.where(lane == sublane + rows, norms[:, 64:65], 0.0))
    own[piece:, :] = jnp.sum(picked, axis=0, keepdims=True)

    for role in range(2):
        drain(data_buf.at[role], first_recv.at[role, 0], 1)
        for d in range(half):
            drain(data_buf.at[role], on_recv.at[role, d], 2)
    def share(offsets):
        for d in offsets:
            for role in range(2):
                block = pair(b + step_of(role) * d)
                remote(
                    data_buf.at[role, block, :, pl.ds(0, shared)], outer_buf.at[role, block, :, pl.ds(0, shared)],
                    outer_send.at[role, 1], outer_recv.at[role, 1], at(wrap(b - step_of(role))),
                )

    offsets = list(range(half + 1))
    share(offsets[:EARLY])

    chunk = min(1024, w)
    for role in range(2):
        for q in range(w // chunk):
            columns = pl.ds(q * chunk, chunk)
            full[role, :, columns] = (
                data_buf[role, :, :, columns].astype(jnp.float32).reshape(total, chunk).astype(jnp.bfloat16)
            )
    for role in range(2):
        drain(noise_buf.at[role], noise_recv.at[role], nb // 2 - 1)

    served = total // 2
    for role in range(2):
        acc = jnp.zeros((served, total), jnp.float32)
        for q in range(w // chunk):
            columns = pl.ds(q * chunk, chunk)
            left = noise_buf[role, :, :, columns].astype(jnp.float32).reshape(served, chunk).astype(jnp.bfloat16)
            acc = acc + lax.dot_general(
                left, full[role, :, columns], (((1,), (1,)), ((), ())), preferred_element_type=jnp.float32
            )
        acc = acc.reshape(half, 2, rows, total)
        for d in range(half):
            block = pair(b - step_of(role) * d)
            if role and not d:
                part[block] = part[block] + acc[d]
            else:
                part[block] = acc[d]
    part[pair(b + nb // 2)] = jnp.zeros((2, rows, total), jnp.float32)

    part_of = part.reshape(nf, piece, total) if piece != rows else part
    a_buf[f] = part_of[f]
    exchange(lambda k: part_of.at[lax.rem(f + k, nf)], a_buf, f, in_plane, f_order, 1)
    drain(a_buf, small_recv.at[1], nf - 1)
    own[:piece, :] = jnp.sum(a_buf[...], axis=0)
    b_buf[b] = own[...]
    exchange(lambda k: own, b_buf, b, in_column, b_order, 2)
    share(offsets[EARLY:])
    drain(b_buf, small_recv.at[2], nb - 1)
    done[...] = jnp.sum(b_buf[:, :piece, :], axis=0)
    c_buf[f] = done[...]
    exchange(lambda k: done, c_buf, f, in_plane, f_order, 3)
    norms = jnp.broadcast_to(b_buf[:, piece:, :], (nb, rows, 128))
    noise_norm = jnp.sum(jnp.where(lane == sublane, norms, 0.0), axis=2, keepdims=True).reshape(total, 1)
    data_norm = jnp.sum(jnp.where(lane == sublane + rows, norms, 0.0), axis=2, keepdims=True).reshape(total, 1)
    data_norm = jnp.transpose(jnp.broadcast_to(data_norm, (total, 128)))[:1, :]
    drain(c_buf, small_recv.at[3], nf - 1)
    cross = c_buf[...].reshape(total, total)

    scores = (2.0 * cross - noise_norm - data_norm) / root + 2.0 * root
    column = jnp.zeros((1, total), jnp.float32)
    for _ in range(ITERS):
        row = -log_count - lse(scores + column, 1)
        column = -log_count - lse(scores + row, 0)
    plan = jnp.exp(scores + row + column)
    weights = plan / jnp.sum(plan, axis=1, keepdims=True)
    wbuf[...] = weights.reshape(nb, rows, total)

    parts = 2
    step = math.gcd(512, shared // parts)
    kept = []

    def targets(chips, role, values, buf, first, count):
        blocks = []
        for d in chips:
            blocks += [wrap(sibling - step_of(role) * d), wrap(b - step_of(role) * d)]
        chosen = jnp.concatenate([wbuf[t] for t in blocks], axis=0).astype(jnp.bfloat16)
        for q in range(first, first + count, step):
            summed = jnp.dot(chosen, values[role, :, q:q + step], preferred_element_type=jnp.float32)
            buf[role, :len(blocks), :, q:q + step] = summed.reshape(len(blocks), rows, step).astype(jnp.bfloat16)

    def to_own(buf, role, place, slice_at, first, count, sem):
        where = columns_of(slice_at, first, count)
        remote(
            buf.at[role, place, :, pl.ds(first, count)], out.at[:, where],
            out_send.at[sem], out_recv.at[sem], at(sibling),
        )
        c = pltpu.make_async_copy(
            buf.at[role, place + 1, :, pl.ds(first, count)], out.at[:, where], local_sem.at[sem]
        )
        c.start()
        kept.append(c)

    def to_chips(chips, buf, slice_of, first, count, sem, roles):
        for q in range(nb // 2):
            for role in roles:
                d = lax.rem((b // 2 - q if role == 0 else q - b // 2) + nb, nb // 2)

                @pl.when((d >= max(chips[-1], 1)) & (d <= chips[0]))
                def _(q=q, role=role, d=d):
                    where = columns_of(slice_of(role, b), first, count)
                    for i, t in enumerate((2 * q + 1 - core, 2 * q + core)):
                        place = 2 * (chips[0] - d) + i
                        remote(
                            buf.at[role, place, :, pl.ds(first, count)], out.at[:, where],
                            out_send.at[sem + role], out_recv.at[sem + role], at(t),
                        )

    far = list(range(half - 1, -1, -1))
    groups = []
    if shared < w:
        for role in range(2):
            targets(far, role, full, obuf, shared, w - shared)
        to_chips(far, obuf, slice_for, shared, w - shared, 0, (0, 1))
        for role in range(2):
            to_own(obuf, role, nb // 2 - 2, slice_for(role, b), shared, w - shared, role)
            groups.append((role, shared, w - shared, nb // 2 - 1))
    for role in range(2):
        targets([0], role, full, obuf, 0, shared)
        to_own(obuf, role, 0, slice_for(role, b), 0, shared, 2 + role)
        groups.append((2 + role, 0, shared, 1))
    for role in range(2):
        drain(outer_buf.at[role], outer_recv.at[role, 0], 1)
        view = outer_buf.at[role, pl.ds(0, 2 * len(offsets)), :, pl.ds(0, shared)]
        pltpu.make_async_copy(view, view, outer_recv.at[role, 1]).wait()
    n = shared // parts
    for g in range(parts):
        for role in range(2):
            for q in range(g * n, (g + 1) * n, step):
                columns = pl.ds(q, step)
                outer_full[role, :, columns] = (
                    outer_buf[role, :, :, columns].astype(jnp.float32).reshape(total, step).astype(jnp.bfloat16)
                )
            targets(far[1:], role, outer_full, outer_obuf, g * n, n)
        sem = 4 + 2 * g
        to_chips(far[1:], outer_obuf, outer_slice, g * n, n, sem, (0, 1))
        for role in range(2):
            to_own(outer_obuf, role, nb // 2 - 4, outer_slice(role, b), g * n, n, sem + role)
            groups.append((sem + role, g * n, n, nb // 2 - 3))

    col_out[...] = column
    pot[...] = jnp.broadcast_to(row, (total, 128)).reshape(nb, rows, 128)
    row_out[...] = jnp.sum(jnp.where(lane == sublane, pot[b], 0.0), axis=0, keepdims=True)[:, :rows]

    for role in range(2):
        for d in range(half):
            drain(data_buf.at[role], first_send.at[role, d], 2 if d else 1)
            drain(data_buf.at[role], on_send.at[role, d], 2)
        for d in range(half - 1, 1, -1):
            drain(data_buf.at[role], outer_send.at[role, d], 2)
        drain(outer_buf.at[role], outer_send.at[role, 0], 1)
        view = outer_buf.at[role, pl.ds(0, 2 * len(offsets)), :, pl.ds(0, shared)]
        pltpu.make_async_copy(view, view, outer_send.at[role, 1]).wait()
        drain(noise_buf.at[role], noise_send.at[role], nb // 2 - 1)
    drain(norm_b, small_send.at[0], nf - 1)
    drain(a_buf, small_send.at[1], nf - 1)
    drain(b_buf, small_send.at[2], nb - 1)
    drain(c_buf, small_send.at[3], nf - 1)
    for sem, first, count, blocks in groups:
        view = obuf.at[0, pl.ds(0, blocks), :, pl.ds(first, count)]
        pltpu.make_async_copy(view, view, out_send.at[sem]).wait()
        pltpu.make_async_copy(view, view, out_recv.at[sem]).wait()
    for c in kept:
        c.wait()


def solution(mesh):
    nb, nf = mesh.shape["batch"], mesh.shape["feat"]

    def per_device(noise, data):
        rows, width = noise.shape
        total, w = rows * nb, width // nb
        piece = total // nf
        targets, row, column = pl.pallas_call(
            functools.partial(kernel, nb, nf),
            out_shape=(
                jax.ShapeDtypeStruct((rows, width), jnp.bfloat16),
                jax.ShapeDtypeStruct((1, rows), jnp.float32),
                jax.ShapeDtypeStruct((1, total), jnp.float32),
            ),
            in_specs=[pl.BlockSpec(memory_space=pl.ANY)] * 2,
            out_specs=[pl.BlockSpec(memory_space=pltpu.VMEM)] * 3,
            scratch_shapes=[
                pltpu.VMEM((2, nb // 2, rows, w), jnp.bfloat16),
                pltpu.VMEM((2, nb, rows, w), jnp.bfloat16),
                pltpu.VMEM((2, nb, rows, w), jnp.bfloat16),
                pltpu.VMEM((2, total, w), jnp.bfloat16),
                pltpu.VMEM((2, total, w), jnp.bfloat16),
                pltpu.VMEM((2, rows, width), jnp.bfloat16),
                pltpu.VMEM((2, nb // 2, rows, w), jnp.bfloat16),
                pltpu.VMEM((2, nb // 2 - 2, rows, w), jnp.bfloat16),
                pltpu.VMEM((nb, rows, total), jnp.float32),
                pltpu.VMEM((nf, piece, total), jnp.float32),
                pltpu.VMEM((piece + 1, total), jnp.float32),
                pltpu.VMEM((nb, piece + 1, total), jnp.float32),
                pltpu.VMEM((piece, total), jnp.float32),
                pltpu.VMEM((nf, piece, total), jnp.float32),
                pltpu.VMEM((rows, 128), jnp.float32),
                pltpu.VMEM((nf, rows, 128), jnp.float32),
                pltpu.VMEM((nb, rows, 128), jnp.float32),
                pltpu.VMEM((nb, rows, total), jnp.float32),
                pltpu.SemaphoreType.DMA((8,)),
                pltpu.SemaphoreType.DMA((2, nb // 4)),
                pltpu.SemaphoreType.DMA((2, nb // 4)),
                pltpu.SemaphoreType.DMA((2, nb // 4)),
                pltpu.SemaphoreType.DMA((2, nb // 4)),
                pltpu.SemaphoreType.DMA((2,)),
                pltpu.SemaphoreType.DMA((2,)),
                pltpu.SemaphoreType.DMA((2, nb // 4)),
                pltpu.SemaphoreType.DMA((2, nb // 4)),
                pltpu.SemaphoreType.DMA((4,)),
                pltpu.SemaphoreType.DMA((4,)),
                pltpu.SemaphoreType.DMA((8,)),
                pltpu.SemaphoreType.DMA((8,)),
                pltpu.SemaphoreType.REGULAR((6,)),
            ],
            compiler_params=pltpu.CompilerParams(
                collective_id=0, has_side_effects=True, vmem_limit_bytes=52 * 2**20
            ),
        )(noise, data)
        return targets, row.reshape(rows), column.reshape(total)

    return jax.shard_map(
        per_device,
        mesh=mesh,
        in_specs=(P("batch", "feat"), P("batch", "feat")),
        out_specs=(P("batch", "feat"), P("batch"), P()),
        check_vma=False,
    )
```

```python
import functools
import math

import jax
import jax.numpy as jnp
from jax import lax
from jax.experimental import pallas as pl
from jax.experimental.pallas import tpu as pltpu
from jax.sharding import PartitionSpec as P

ITERS = 3
SHARED = 7
EARLY = 2
MESH = pl.DeviceIdType.MESH


def lse(values, axis):
    top = jnp.max(values, axis=axis, keepdims=True)
    return top + jnp.log(jnp.sum(jnp.exp(values - top), axis=axis, keepdims=True))


def far_first(count):
    return sorted(range(1, count), key=lambda k: (-min(k, count - k), k))


def kernel(
    nb, nf, noise, data, out, row_out, col_out,
    noise_buf, data_buf, outer_buf, full, outer_full, local_buf, obuf, outer_obuf,
    part, a_buf, own, b_buf, done, c_buf, norm_own, norm_b, pot, wbuf,
    local_sem, outer_send, outer_recv, first_send, first_recv, noise_send, noise_recv, on_send, on_recv,
    small_send, small_recv, out_send, out_recv, arrived,
):
    rows, width = noise.shape
    w = width // nb
    total = rows * nb
    piece = total // nf
    features = width * nf
    root = math.sqrt(features)
    log_count = math.log(total)
    half = nb // 4
    shared = w * SHARED // 8
    b, f = lax.axis_index("batch"), lax.axis_index("feat")
    core = lax.rem(b, 2)
    sibling = b + 1 - 2 * core
    b_order, f_order = far_first(nb), list(range(1, nf))

    def at(t):
        return dict(device_id=(t, f), device_id_type=MESH)

    def in_column(k):
        return at(lax.rem(b + k, nb))

    def in_plane(k):
        return dict(device_id=(b, lax.rem(f + k, nf)), device_id_type=MESH)

    def drain(ref, sem, count):
        view = ref.at[pl.ds(0, count)]
        pltpu.make_async_copy(view, view, sem).wait()

    def wrap(t):
        return lax.rem(t + 2 * nb, nb)

    def pair(device):
        return pl.ds(pl.multiple_of(wrap(device) // 2 * 2, 2), 2)

    def columns_of(slice_at, q=0, n=w):
        return pl.ds(pl.multiple_of(slice_at * w + q, math.gcd(w, q)), n)

    def step_of(role):
        return 2 if role == 0 else -2

    def slice_for(role, member):
        return wrap(member - 2 * role)

    def outer_slice(role, device):
        return slice_for(role, wrap(device + step_of(role)))

    def remote(source, target, send, recv, device):
        pltpu.make_async_remote_copy(
            src_ref=source, dst_ref=target, send_sem=send, recv_sem=recv, **device
        ).start()

    side = math.isqrt(nf)
    fy, fx = f // side, lax.rem(f, side)

    def in_grid(y, x):
        place = lax.rem(fy + y + side, side) * side + lax.rem(fx + x + side, side)
        return dict(device_id=(b, place), device_id_type=MESH)

    beside = [in_column(2), in_column(nb - 2)]
    diagonal = [at(wrap(sibling + 2)), at(wrap(sibling - 2))]
    row_beside = [in_grid(0, 1), in_grid(0, -1)]
    column_beside = [in_grid(1, 0), in_grid(-1, 0)]
    barrier = pltpu.get_barrier_semaphore()
    near = beside + diagonal + [at(sibling)] + row_beside + column_beside
    for device in near:
        pl.semaphore_signal(barrier, inc=1, **device)
    pl.semaphore_wait(barrier, len(near))

    def tell(devices, which):
        for device in devices:
            pl.semaphore_signal(arrived.at[which], inc=1, **device)

    tell(beside, 0)
    tell(row_beside, 3)

    for role in range(2):
        for member in (b, sibling):
            remote(
                data.at[:, columns_of(slice_for(role, member))], data_buf.at[1 - role, b],
                on_send.at[role, 0], on_recv.at[1 - role, 0], at(wrap(member + step_of(role))),
            )
    def send_data(d):
        for role in range(2):
            for member in [sibling] if d == 0 else [
                wrap(b + step_of(role) * d), wrap(sibling + step_of(role) * d)
            ]:
                source = data.at[:, columns_of(slice_for(role, member))]
                if d > 1:
                    remote(
                        source, outer_buf.at[role, b],
                        first_send.at[role, d], outer_recv.at[role, d], at(wrap(member - step_of(role))),
                    )
                else:
                    remote(
                        source, data_buf.at[role, b], first_send.at[role, d], first_recv.at[role, d], at(member)
                    )
    send_data(2)
    pl.semaphore_wait(arrived.at[0], 2)
    tell(beside, 1)
    for d in (3, 1, 0):
        send_data(d)
    locals_ = []
    for role in range(2):
        s = columns_of(slice_for(role, b))
        locals_.append(pltpu.make_async_copy(data.at[:, s], data_buf.at[role, b], local_sem.at[role]))
        locals_.append(pltpu.make_async_copy(noise.at[:, s], noise_buf.at[role, core], local_sem.at[2 + role]))
        s = columns_of(outer_slice(role, b))
        locals_.append(pltpu.make_async_copy(data.at[:, s], outer_buf.at[role, b], local_sem.at[6 + role]))
    locals_.append(pltpu.make_async_copy(noise, local_buf.at[0], local_sem.at[4]))
    locals_.append(pltpu.make_async_copy(data, local_buf.at[1], local_sem.at[5]))
    for c in locals_:
        c.start()
    for role in range(2):
        remote(
            data.at[:, columns_of(outer_slice(role, sibling))], outer_buf.at[role, b],
            outer_send.at[role, 0], outer_recv.at[role, 0], at(sibling),
        )

    def send_noise(distances):
        for d in distances:
            for role in range(2):
                for member in [sibling] if d == 0 else [
                    wrap(b + step_of(role) * d), wrap(sibling + step_of(role) * d)
                ]:
                    remote(
                        noise.at[:, columns_of(slice_for(role, member))], noise_buf.at[role, 2 * d + core],
                        noise_send.at[role], noise_recv.at[role], at(member),
                    )

    pl.semaphore_wait(arrived.at[3], 2)
    tell(column_beside, 4)
    pl.semaphore_wait(arrived.at[1], 2)
    tell(beside, 2)
    send_noise([half - 1])
    pl.semaphore_wait(arrived.at[4], 2)
    tell(column_beside, 5)
    pl.semaphore_wait(arrived.at[2], 2)
    pl.semaphore_wait(arrived.at[5], 2)
    for c in locals_:
        c.wait()

    def exchange(src_of, buf, slot, partner, order, sem):
        for k in order:
            remote(src_of(k), buf.at[slot], small_send.at[sem], small_recv.at[sem], partner(k))

    chunk = min(2048, width)
    sums = []
    for i in range(2):
        def add(step, acc, i=i):
            v = local_buf[i, :, pl.ds(pl.multiple_of(step * chunk, chunk), chunk)].astype(jnp.float32)
            v = v * v
            for q in range(chunk // 128):
                acc = acc + v[:, q * 128:(q + 1) * 128]
            return acc
        acc = lax.fori_loop(0, width // chunk, add, jnp.zeros((rows, 128), jnp.float32))
        sums.append(jnp.sum(acc, axis=1, keepdims=True))
    lane = lax.broadcasted_iota(jnp.int32, (rows, 128), 1)
    sublane = lax.broadcasted_iota(jnp.int32, (rows, 128), 0)
    norm_own[...] = jnp.where(lane < 64, sums[0], sums[1])
    norm_b[f] = norm_own[...]
    exchange(lambda k: norm_own, norm_b, f, in_plane, f_order, 0)

    def onward(d):
        for role in range(2):
            drain(data_buf.at[role], first_recv.at[role, d], 2)
            block = pair(b - step_of(role) * d)
            remote(
                data_buf.at[role, block], data_buf.at[1 - role, block],
                on_send.at[role, d], on_recv.at[1 - role, d], at(wrap(b + step_of(role))),
            )

    for d in range(half - 1, 1, -1):
        for role in range(2):
            drain(outer_buf.at[role], outer_recv.at[role, d], 2)
            block = pair(b - step_of(role) * (d - 1))
            remote(
                outer_buf.at[role, block], data_buf.at[role, block],
                outer_send.at[role, d], first_recv.at[role, d], at(wrap(b + step_of(role))),
            )
    onward(1)
    send_noise(range(half - 2, 1, -1))
    for d in range(half - 1, 1, -1):
        onward(d)
    send_noise([1, 0])

    drain(norm_b, small_recv.at[0], nf - 1)
    norms = jnp.sum(norm_b[...], axis=0)
    picked = jnp.where(lane == sublane, norms[:, :1], jnp.where(lane == sublane + rows, norms[:, 64:65], 0.0))
    own[piece:, :] = jnp.sum(picked, axis=0, keepdims=True)

    for role in range(2):
        drain(data_buf.at[role], first_recv.at[role, 0], 1)
        for d in range(half):
            drain(data_buf.at[role], on_recv.at[role, d], 2)
    def share(offsets, sem, first=0, count=shared):
        here = pl.ds(first, count)
        for d in offsets:
            for role in range(2):
                block = pair(b + step_of(role) * d)
                remote(
                    data_buf.at[role, block, :, here], outer_buf.at[role, block, :, here],
                    outer_send.at[role, sem], outer_recv.at[role, sem], at(wrap(b - step_of(role))),
                )

    offsets = list(range(half + 1))
    early, late = offsets[:EARLY], offsets[EARLY:]
    share(early, 1)
    share(late[:1], half, 0, shared // 2)

    chunk = min(1024, w)
    for role in range(2):
        for q in range(w // chunk):
            columns = pl.ds(q * chunk, chunk)
            full[role, :, columns] = (
                data_buf[role, :, :, columns].astype(jnp.float32).reshape(total, chunk).astype(jnp.bfloat16)
            )
    for role in range(2):
        drain(noise_buf.at[role], noise_recv.at[role], nb // 2 - 1)

    served = total // 2
    accs = [jnp.zeros((served, total), jnp.float32)] * 2
    chunk = min(1024, w)
    for q in range(w // chunk):
        columns = pl.ds(q * chunk, chunk)
        for role in range(2):
            left = noise_buf[role, :, :, columns].astype(jnp.float32).reshape(served, chunk).astype(jnp.bfloat16)
            accs[role] = accs[role] + lax.dot_general(
                left, full[role, :, columns], (((1,), (1,)), ((), ())), preferred_element_type=jnp.float32
            )
    for role in range(2):
        acc = accs[role].reshape(half, 2, rows, total)
        for d in range(half):
            block = pair(b - step_of(role) * d)
            if role and not d:
                part[block] = part[block] + acc[d]
            else:
                part[block] = acc[d]
    part[pair(b + nb // 2)] = jnp.zeros((2, rows, total), jnp.float32)

    part_of = part.reshape(nf, piece, total) if piece != rows else part
    a_buf[f] = part_of[f]
    exchange(lambda k: part_of.at[lax.rem(f + k, nf)], a_buf, f, in_plane, f_order, 1)
    drain(a_buf, small_recv.at[1], nf - 1)
    own[:piece, :] = jnp.sum(a_buf[...], axis=0)
    b_buf[b] = own[...]
    exchange(lambda k: own, b_buf, b, in_column, b_order, 2)
    share(late[:1], half, shared // 2, shared // 2)
    share(late[1:], half)

    def outer_pairs(devices, roles=(0, 1)):
        for role in roles:
            for device in devices(role):
                block = pair(device)
                at_row = pl.ds(pl.multiple_of(wrap(device) // 2 * (2 * rows), 2 * rows), 2 * rows)
                outer_full[role, at_row, :shared] = (
                    outer_buf[role, block, :, :shared].astype(jnp.float32)
                    .reshape(2 * rows, shared).astype(jnp.bfloat16)
                )

    def arrival(kind, sem, count, roles=(0, 1)):
        for role in roles:
            view = outer_buf.at[role, pl.ds(0, 2 * count), :, pl.ds(0, shared)]
            pltpu.make_async_copy(view, view, kind.at[role, sem]).wait()

    for role in range(2):
        drain(outer_buf.at[role], outer_recv.at[role, 0], 1)
    outer_pairs(lambda role: [b - step_of(role) * d for d in range(half - 1)])
    drain(b_buf, small_recv.at[2], nb - 1)
    done[...] = jnp.sum(b_buf[:, :piece, :], axis=0)
    c_buf[f] = done[...]
    exchange(lambda k: done, c_buf, f, in_plane, f_order, 3)
    norms = jnp.broadcast_to(b_buf[:, piece:, :], (nb, rows, 128))
    noise_norm = jnp.sum(jnp.where(lane == sublane, norms, 0.0), axis=2, keepdims=True).reshape(total, 1)
    data_norm = jnp.sum(jnp.where(lane == sublane + rows, norms, 0.0), axis=2, keepdims=True).reshape(total, 1)
    data_norm = jnp.transpose(jnp.broadcast_to(data_norm, (total, 128)))[:1, :]
    arrival(outer_recv, 1, len(early))
    outer_pairs(lambda role: [b + step_of(role) * (d + 1) for d in early])
    drain(c_buf, small_recv.at[3], nf - 1)
    cross = c_buf[...].reshape(total, total)

    scores = (2.0 * cross - noise_norm - data_norm) / root + 2.0 * root
    column = jnp.zeros((1, total), jnp.float32)
    for _ in range(ITERS):
        row = -log_count - lse(scores + column, 1)
        column = -log_count - lse(scores + row, 0)
    plan = jnp.exp(scores + row + column)
    weights = plan / jnp.sum(plan, axis=1, keepdims=True)
    wbuf[...] = weights.reshape(nb, rows, total)

    step = math.gcd(512, shared)
    kept = []

    def targets(chips, role, values, buf, first, count):
        blocks = []
        for d in chips:
            blocks += [wrap(sibling - step_of(role) * d), wrap(b - step_of(role) * d)]
        chosen = jnp.concatenate([wbuf[t] for t in blocks], axis=0).astype(jnp.bfloat16)
        for q in range(first, first + count, step):
            summed = jnp.dot(chosen, values[role, :, q:q + step], preferred_element_type=jnp.float32)
            buf[role, :len(blocks), :, q:q + step] = summed.reshape(len(blocks), rows, step).astype(jnp.bfloat16)

    def to_own(buf, role, place, slice_at, first, count, sem):
        where = columns_of(slice_at, first, count)
        remote(
            buf.at[role, place, :, pl.ds(first, count)], out.at[:, where],
            out_send.at[sem], out_recv.at[sem], at(sibling),
        )
        c = pltpu.make_async_copy(
            buf.at[role, place + 1, :, pl.ds(first, count)], out.at[:, where], local_sem.at[sem]
        )
        c.start()
        kept.append(c)

    def to_chips(chips, buf, slice_of, first, count, sem, roles):
        for q in range(nb // 2):
            for role in roles:
                d = lax.rem((b // 2 - q if role == 0 else q - b // 2) + nb, nb // 2)

                @pl.when((d >= max(chips[-1], 1)) & (d <= chips[0]))
                def _(q=q, role=role, d=d):
                    where = columns_of(slice_of(role, b), first, count)
                    for i, t in enumerate((2 * q + 1 - core, 2 * q + core)):
                        place = 2 * (chips[0] - d) + i
                        remote(
                            buf.at[role, place, :, pl.ds(first, count)], out.at[:, where],
                            out_send.at[sem + role], out_recv.at[sem + role], at(t),
                        )

    far = list(range(half - 1, -1, -1))
    for role in range(2):
        targets(far, role, full, obuf, shared, w - shared)
    to_chips(far, obuf, slice_for, shared, w - shared, 0, (0, 1))
    for role in range(2):
        arrival(outer_recv, half, len(late), (role,))
        outer_pairs(lambda role: [b + step_of(role) * (d + 1) for d in late], (role,))
        targets(far[1:], role, outer_full, outer_obuf, 0, shared)
        to_chips(far[1:], outer_obuf, outer_slice, 0, shared, 4, (role,))
    for role in range(2):
        to_own(outer_obuf, role, nb // 2 - 4, outer_slice(role, b), 0, shared, 4 + role)
        to_own(obuf, role, nb // 2 - 2, slice_for(role, b), shared, w - shared, role)
        targets([0], role, full, obuf, 0, shared)
        to_own(obuf, role, 0, slice_for(role, b), 0, shared, 2 + role)
    groups = [
        (role + sem, first, count, blocks)
        for role in range(2)
        for sem, first, count, blocks in (
            (0, shared, w - shared, nb // 2 - 1), (2, 0, shared, 1), (4, 0, shared, nb // 2 - 3)
        )
    ]

    col_out[...] = column
    pot[...] = jnp.broadcast_to(row, (total, 128)).reshape(nb, rows, 128)
    row_out[...] = jnp.sum(jnp.where(lane == sublane, pot[b], 0.0), axis=0, keepdims=True)[:, :rows]

    for role in range(2):
        for d in range(half):
            drain(data_buf.at[role], first_send.at[role, d], 2 if d else 1)
            drain(data_buf.at[role], on_send.at[role, d], 2)
        for d in range(half - 1, 1, -1):
            drain(data_buf.at[role], outer_send.at[role, d], 2)
        drain(outer_buf.at[role], outer_send.at[role, 0], 1)
        drain(noise_buf.at[role], noise_send.at[role], nb // 2 - 1)
    arrival(outer_send, 1, len(early))
    arrival(outer_send, half, len(late))
    drain(norm_b, small_send.at[0], nf - 1)
    drain(a_buf, small_send.at[1], nf - 1)
    drain(b_buf, small_send.at[2], nb - 1)
    drain(c_buf, small_send.at[3], nf - 1)
    for sem, first, count, blocks in groups:
        view = obuf.at[0, pl.ds(0, blocks), :, pl.ds(first, count)]
        pltpu.make_async_copy(view, view, out_send.at[sem]).wait()
        pltpu.make_async_copy(view, view, out_recv.at[sem]).wait()
    for c in kept:
        c.wait()


def solution(mesh):
    nb, nf = mesh.shape["batch"], mesh.shape["feat"]

    def per_device(noise, data):
        rows, width = noise.shape
        total, w = rows * nb, width // nb
        piece = total // nf
        targets, row, column = pl.pallas_call(
            functools.partial(kernel, nb, nf),
            out_shape=(
                jax.ShapeDtypeStruct((rows, width), jnp.bfloat16),
                jax.ShapeDtypeStruct((1, rows), jnp.float32),
                jax.ShapeDtypeStruct((1, total), jnp.float32),
            ),
            in_specs=[pl.BlockSpec(memory_space=pl.ANY)] * 2,
            out_specs=[pl.BlockSpec(memory_space=pltpu.VMEM)] * 3,
            scratch_shapes=[
                pltpu.VMEM((2, nb // 2, rows, w), jnp.bfloat16),
                pltpu.VMEM((2, nb, rows, w), jnp.bfloat16),
                pltpu.VMEM((2, nb, rows, w), jnp.bfloat16),
                pltpu.VMEM((2, total, w), jnp.bfloat16),
                pltpu.VMEM((2, total, w), jnp.bfloat16),
                pltpu.VMEM((2, rows, width), jnp.bfloat16),
                pltpu.VMEM((2, nb // 2, rows, w), jnp.bfloat16),
                pltpu.VMEM((2, nb // 2 - 2, rows, w), jnp.bfloat16),
                pltpu.VMEM((nb, rows, total), jnp.float32),
                pltpu.VMEM((nf, piece, total), jnp.float32),
                pltpu.VMEM((piece + 1, total), jnp.float32),
                pltpu.VMEM((nb, piece + 1, total), jnp.float32),
                pltpu.VMEM((piece, total), jnp.float32),
                pltpu.VMEM((nf, piece, total), jnp.float32),
                pltpu.VMEM((rows, 128), jnp.float32),
                pltpu.VMEM((nf, rows, 128), jnp.float32),
                pltpu.VMEM((nb, rows, 128), jnp.float32),
                pltpu.VMEM((nb, rows, total), jnp.float32),
                pltpu.SemaphoreType.DMA((8,)),
                pltpu.SemaphoreType.DMA((2, nb // 4 + 1)),
                pltpu.SemaphoreType.DMA((2, nb // 4 + 1)),
                pltpu.SemaphoreType.DMA((2, nb // 4)),
                pltpu.SemaphoreType.DMA((2, nb // 4)),
                pltpu.SemaphoreType.DMA((2,)),
                pltpu.SemaphoreType.DMA((2,)),
                pltpu.SemaphoreType.DMA((2, nb // 4)),
                pltpu.SemaphoreType.DMA((2, nb // 4)),
                pltpu.SemaphoreType.DMA((4,)),
                pltpu.SemaphoreType.DMA((4,)),
                pltpu.SemaphoreType.DMA((8,)),
                pltpu.SemaphoreType.DMA((8,)),
                pltpu.SemaphoreType.REGULAR((6,)),
            ],
            compiler_params=pltpu.CompilerParams(
                collective_id=0, has_side_effects=True, vmem_limit_bytes=52 * 2**20
            ),
        )(noise, data)
        return targets, row.reshape(rows), column.reshape(total)

    return jax.shard_map(
        per_device,
        mesh=mesh,
        in_specs=(P("batch", "feat"), P("batch", "feat")),
        out_specs=(P("batch", "feat"), P("batch"), P()),
        check_vma=False,
    )
```

```python
import functools
import math

import jax
import jax.numpy as jnp
from jax import lax
from jax.experimental import pallas as pl
from jax.experimental.pallas import tpu as pltpu
from jax.sharding import PartitionSpec as P

ITERS = 3
SHARED = 7
EARLY = 2
MESH = pl.DeviceIdType.MESH


def lse(values, axis):
    top = jnp.max(values, axis=axis, keepdims=True)
    return top + jnp.log(jnp.sum(jnp.exp(values - top), axis=axis, keepdims=True))


def plane_order(side):
    steps = [(y, x) for y in range(side) for x in range(side) if y or x]
    return sorted(steps, key=lambda s: -min(s[0], side - s[0]) - min(s[1], side - s[1]))


def far_first(count):
    return sorted(range(1, count), key=lambda k: (-min(k, count - k), k))


def kernel(
    nb, nf, noise, data, out, row_out, col_out,
    noise_buf, data_buf, outer_buf, full, outer_full, local_buf, obuf, outer_obuf,
    part, a_buf, own, b_buf, done, c_buf, norm_own, norm_b, pot, wbuf,
    local_sem, outer_send, outer_recv, first_send, first_recv, noise_send, noise_recv, on_send, on_recv,
    small_send, small_recv, out_send, out_recv, arrived,
):
    rows, width = noise.shape
    w = width // nb
    total = rows * nb
    piece = total // nf
    features = width * nf
    root = math.sqrt(features)
    log_count = math.log(total)
    half = nb // 4
    shared = w * SHARED // 8
    b, f = lax.axis_index("batch"), lax.axis_index("feat")
    core = lax.rem(b, 2)
    sibling = b + 1 - 2 * core
    side = math.isqrt(nf)
    b_order, f_order = far_first(nb), plane_order(side)
    fy, fx = f // side, lax.rem(f, side)

    def at(t):
        return dict(device_id=(t, f), device_id_type=MESH)

    def in_column(k):
        return at(lax.rem(b + k, nb))

    def place_at(y, x):
        return lax.rem(fy + y + side, side) * side + lax.rem(fx + x + side, side)

    def in_grid(y, x):
        return dict(device_id=(b, place_at(y, x)), device_id_type=MESH)

    def in_plane(k):
        return in_grid(*k)

    def drain(ref, sem, count):
        view = ref.at[pl.ds(0, count)]
        pltpu.make_async_copy(view, view, sem).wait()

    def wrap(t):
        return lax.rem(t + 2 * nb, nb)

    def pair(device):
        return pl.ds(pl.multiple_of(wrap(device) // 2 * 2, 2), 2)

    def columns_of(slice_at, q=0, n=w):
        return pl.ds(pl.multiple_of(slice_at * w + q, math.gcd(w, q)), n)

    def step_of(role):
        return 2 if role == 0 else -2

    def slice_for(role, member):
        return wrap(member - 2 * role)

    def outer_slice(role, device):
        return slice_for(role, wrap(device + step_of(role)))

    def remote(source, target, send, recv, device):
        pltpu.make_async_remote_copy(
            src_ref=source, dst_ref=target, send_sem=send, recv_sem=recv, **device
        ).start()

    beside = [in_column(2), in_column(nb - 2)]
    diagonal = [at(wrap(sibling + 2)), at(wrap(sibling - 2))]
    row_beside = [in_grid(0, 1), in_grid(0, -1)]
    column_beside = [in_grid(1, 0), in_grid(-1, 0)]
    barrier = pltpu.get_barrier_semaphore()
    near = beside + diagonal + [at(sibling)] + row_beside + column_beside
    for device in near:
        pl.semaphore_signal(barrier, inc=1, **device)
    pl.semaphore_wait(barrier, len(near))

    def tell(devices, which):
        for device in devices:
            pl.semaphore_signal(arrived.at[which], inc=1, **device)

    tell(beside, 0)
    tell(row_beside, 3)

    for role in range(2):
        for member in (b, sibling):
            remote(
                data.at[:, columns_of(slice_for(role, member))], data_buf.at[1 - role, b],
                on_send.at[role, 0], on_recv.at[1 - role, 0], at(wrap(member + step_of(role))),
            )
    def send_data(d):
        for role in range(2):
            for member in [sibling] if d == 0 else [
                wrap(b + step_of(role) * d), wrap(sibling + step_of(role) * d)
            ]:
                source = data.at[:, columns_of(slice_for(role, member))]
                if d > 1:
                    remote(
                        source, outer_buf.at[role, b],
                        first_send.at[role, d], outer_recv.at[role, d], at(wrap(member - step_of(role))),
                    )
                else:
                    remote(
                        source, data_buf.at[role, b], first_send.at[role, d], first_recv.at[role, d], at(member)
                    )
    send_data(2)
    pl.semaphore_wait(arrived.at[0], 2)
    tell(beside, 1)
    for d in (3, 1, 0):
        send_data(d)
    locals_ = []
    for role in range(2):
        s = columns_of(slice_for(role, b))
        locals_.append(pltpu.make_async_copy(data.at[:, s], data_buf.at[role, b], local_sem.at[role]))
        locals_.append(pltpu.make_async_copy(noise.at[:, s], noise_buf.at[role, core], local_sem.at[2 + role]))
        s = columns_of(outer_slice(role, b))
        locals_.append(pltpu.make_async_copy(data.at[:, s], outer_buf.at[role, b], local_sem.at[6 + role]))
    locals_.append(pltpu.make_async_copy(noise, local_buf.at[0], local_sem.at[4]))
    locals_.append(pltpu.make_async_copy(data, local_buf.at[1], local_sem.at[5]))
    for c in locals_:
        c.start()
    for role in range(2):
        remote(
            data.at[:, columns_of(outer_slice(role, sibling))], outer_buf.at[role, b],
            outer_send.at[role, 0], outer_recv.at[role, 0], at(sibling),
        )

    def send_noise(distances):
        for d in distances:
            for role in range(2):
                for member in [sibling] if d == 0 else [
                    wrap(b + step_of(role) * d), wrap(sibling + step_of(role) * d)
                ]:
                    remote(
                        noise.at[:, columns_of(slice_for(role, member))], noise_buf.at[role, 2 * d + core],
                        noise_send.at[role], noise_recv.at[role], at(member),
                    )

    pl.semaphore_wait(arrived.at[3], 2)
    tell(column_beside, 4)
    pl.semaphore_wait(arrived.at[1], 2)
    tell(beside, 2)
    send_noise([half - 1])
    pl.semaphore_wait(arrived.at[4], 2)
    tell(column_beside, 5)
    pl.semaphore_wait(arrived.at[2], 2)
    pl.semaphore_wait(arrived.at[5], 2)
    for c in locals_:
        c.wait()

    def exchange(src_of, buf, slot, partner, order, sem):
        for k in order:
            remote(src_of(k), buf.at[slot], small_send.at[sem], small_recv.at[sem], partner(k))

    chunk = min(2048, width)
    sums = []
    for i in range(2):
        def add(step, acc, i=i):
            v = local_buf[i, :, pl.ds(pl.multiple_of(step * chunk, chunk), chunk)].astype(jnp.float32)
            v = v * v
            for q in range(chunk // 128):
                acc = acc + v[:, q * 128:(q + 1) * 128]
            return acc
        acc = lax.fori_loop(0, width // chunk, add, jnp.zeros((rows, 128), jnp.float32))
        sums.append(jnp.sum(acc, axis=1, keepdims=True))
    lane = lax.broadcasted_iota(jnp.int32, (rows, 128), 1)
    sublane = lax.broadcasted_iota(jnp.int32, (rows, 128), 0)
    norm_own[...] = jnp.where(lane < 64, sums[0], sums[1])
    norm_b[f] = norm_own[...]
    exchange(lambda k: norm_own, norm_b, f, in_plane, f_order, 0)

    def onward(d):
        for role in range(2):
            drain(data_buf.at[role], first_recv.at[role, d], 2)
            block = pair(b - step_of(role) * d)
            remote(
                data_buf.at[role, block], data_buf.at[1 - role, block],
                on_send.at[role, d], on_recv.at[1 - role, d], at(wrap(b + step_of(role))),
            )

    for d in range(half - 1, 1, -1):
        for role in range(2):
            drain(outer_buf.at[role], outer_recv.at[role, d], 2)
            block = pair(b - step_of(role) * (d - 1))
            remote(
                outer_buf.at[role, block], data_buf.at[role, block],
                outer_send.at[role, d], first_recv.at[role, d], at(wrap(b + step_of(role))),
            )
    onward(1)
    send_noise(range(half - 2, 1, -1))
    for d in range(half - 1, 1, -1):
        onward(d)
    send_noise([1, 0])

    drain(norm_b, small_recv.at[0], nf - 1)
    norms = jnp.sum(norm_b[...], axis=0)
    picked = jnp.where(lane == sublane, norms[:, :1], jnp.where(lane == sublane + rows, norms[:, 64:65], 0.0))
    own[piece:, :] = jnp.sum(picked, axis=0, keepdims=True)

    for role in range(2):
        drain(data_buf.at[role], first_recv.at[role, 0], 1)
        for d in range(half):
            drain(data_buf.at[role], on_recv.at[role, d], 2)
    def share(offsets, sem, first=0, count=shared):
        here = pl.ds(first, count)
        for d in offsets:
            for role in range(2):
                block = pair(b + step_of(role) * d)
                remote(
                    data_buf.at[role, block, :, here], outer_buf.at[role, block, :, here],
                    outer_send.at[role, sem], outer_recv.at[role, sem], at(wrap(b - step_of(role))),
                )

    offsets = list(range(half + 1))
    early, late = offsets[:EARLY], offsets[EARLY:]
    share(early, 1)
    share(late[:1], half, 0, shared // 2)

    chunk = min(1024, w)
    for role in range(2):
        for q in range(w // chunk):
            columns = pl.ds(q * chunk, chunk)
            full[role, :, columns] = (
                data_buf[role, :, :, columns].astype(jnp.float32).reshape(total, chunk).astype(jnp.bfloat16)
            )
    for role in range(2):
        drain(noise_buf.at[role], noise_recv.at[role], nb // 2 - 1)

    served = total // 2
    accs = [jnp.zeros((served, total), jnp.float32)] * 2
    chunk = min(1024, w)
    for q in range(w // chunk):
        columns = pl.ds(q * chunk, chunk)
        for role in range(2):
            left = noise_buf[role, :, :, columns].astype(jnp.float32).reshape(served, chunk).astype(jnp.bfloat16)
            accs[role] = accs[role] + lax.dot_general(
                left, full[role, :, columns], (((1,), (1,)), ((), ())), preferred_element_type=jnp.float32
            )
    for role in range(2):
        acc = accs[role].reshape(half, 2, rows, total)
        for d in range(half):
            block = pair(b - step_of(role) * d)
            if role and not d:
                part[block] = part[block] + acc[d]
            else:
                part[block] = acc[d]
    part[pair(b + nb // 2)] = jnp.zeros((2, rows, total), jnp.float32)

    part_of = part.reshape(nf, piece, total) if piece != rows else part
    a_buf[f] = part_of[f]
    exchange(lambda k: part_of.at[place_at(*k)], a_buf, f, in_plane, f_order, 1)
    drain(a_buf, small_recv.at[1], nf - 1)
    own[:piece, :] = jnp.sum(a_buf[...], axis=0)
    b_buf[b] = own[...]
    exchange(lambda k: own, b_buf, b, in_column, b_order, 2)
    share(late[:1], half, shared // 2, shared // 2)
    share(late[1:], half)

    def outer_pairs(devices, roles=(0, 1)):
        for role in roles:
            for device in devices(role):
                block = pair(device)
                at_row = pl.ds(pl.multiple_of(wrap(device) // 2 * (2 * rows), 2 * rows), 2 * rows)
                outer_full[role, at_row, :shared] = (
                    outer_buf[role, block, :, :shared].astype(jnp.float32)
                    .reshape(2 * rows, shared).astype(jnp.bfloat16)
                )

    def arrival(kind, sem, count, roles=(0, 1)):
        for role in roles:
            view = outer_buf.at[role, pl.ds(0, 2 * count), :, pl.ds(0, shared)]
            pltpu.make_async_copy(view, view, kind.at[role, sem]).wait()

    for role in range(2):
        drain(outer_buf.at[role], outer_recv.at[role, 0], 1)
    outer_pairs(lambda role: [b - step_of(role) * d for d in range(half - 1)])
    drain(b_buf, small_recv.at[2], nb - 1)
    done[...] = jnp.sum(b_buf[:, :piece, :], axis=0)
    c_buf[f] = done[...]
    exchange(lambda k: done, c_buf, f, in_plane, f_order, 3)
    norms = jnp.broadcast_to(b_buf[:, piece:, :], (nb, rows, 128))
    noise_norm = jnp.sum(jnp.where(lane == sublane, norms, 0.0), axis=2, keepdims=True).reshape(total, 1)
    data_norm = jnp.sum(jnp.where(lane == sublane + rows, norms, 0.0), axis=2, keepdims=True).reshape(total, 1)
    data_norm = jnp.transpose(jnp.broadcast_to(data_norm, (total, 128)))[:1, :]
    arrival(outer_recv, 1, len(early))
    outer_pairs(lambda role: [b + step_of(role) * (d + 1) for d in early])
    drain(c_buf, small_recv.at[3], nf - 1)
    cross = c_buf[...].reshape(total, total)

    scores = (2.0 * cross - noise_norm - data_norm) / root + 2.0 * root
    column = jnp.zeros((1, total), jnp.float32)
    for _ in range(ITERS):
        row = -log_count - lse(scores + column, 1)
        column = -log_count - lse(scores + row, 0)
    plan = jnp.exp(scores + row + column)
    weights = plan / jnp.sum(plan, axis=1, keepdims=True)
    wbuf[...] = weights.reshape(nb, rows, total)

    step = math.gcd(512, shared)
    kept = []

    def targets(chips, role, values, buf, first, count):
        blocks = []
        for d in chips:
            blocks += [wrap(sibling - step_of(role) * d), wrap(b - step_of(role) * d)]
        chosen = jnp.concatenate([wbuf[t] for t in blocks], axis=0).astype(jnp.bfloat16)
        for q in range(first, first + count, step):
            summed = jnp.dot(chosen, values[role, :, q:q + step], preferred_element_type=jnp.float32)
            buf[role, :len(blocks), :, q:q + step] = summed.reshape(len(blocks), rows, step).astype(jnp.bfloat16)

    def to_own(buf, role, place, slice_at, first, count, sem):
        where = columns_of(slice_at, first, count)
        remote(
            buf.at[role, place, :, pl.ds(first, count)], out.at[:, where],
            out_send.at[sem], out_recv.at[sem], at(sibling),
        )
        c = pltpu.make_async_copy(
            buf.at[role, place + 1, :, pl.ds(first, count)], out.at[:, where], local_sem.at[sem]
        )
        c.start()
        kept.append(c)

    def to_chips(chips, buf, slice_of, first, count, sem, roles):
        for q in range(nb // 2):
            for role in roles[::-1]:
                d = lax.rem((b // 2 - q if role == 0 else q - b // 2) + nb, nb // 2)

                @pl.when((d >= max(chips[-1], 1)) & (d <= chips[0]))
                def _(q=q, role=role, d=d):
                    where = columns_of(slice_of(role, b), first, count)
                    for i, t in enumerate((2 * q + 1 - core, 2 * q + core)):
                        place = 2 * (chips[0] - d) + i
                        remote(
                            buf.at[role, place, :, pl.ds(first, count)], out.at[:, where],
                            out_send.at[sem + role], out_recv.at[sem + role], at(t),
                        )

    far = list(range(half - 1, -1, -1))
    for role in range(2):
        targets(far, role, full, obuf, shared, w - shared)
    to_chips(far, obuf, slice_for, shared, w - shared, 0, (0, 1))
    for role in range(2):
        arrival(outer_recv, half, len(late), (role,))
        outer_pairs(lambda role: [b + step_of(role) * (d + 1) for d in late], (role,))
        targets(far[1:], role, outer_full, outer_obuf, 0, shared)
        to_chips(far[1:], outer_obuf, outer_slice, 0, shared, 4, (role,))
    for role in range(2):
        to_own(outer_obuf, role, nb // 2 - 4, outer_slice(role, b), 0, shared, 4 + role)
        to_own(obuf, role, nb // 2 - 2, slice_for(role, b), shared, w - shared, role)
        targets([0], role, full, obuf, 0, shared)
        to_own(obuf, role, 0, slice_for(role, b), 0, shared, 2 + role)
    groups = [
        (role + sem, first, count, blocks)
        for role in range(2)
        for sem, first, count, blocks in (
            (0, shared, w - shared, nb // 2 - 1), (2, 0, shared, 1), (4, 0, shared, nb // 2 - 3)
        )
    ]

    col_out[...] = column
    pot[...] = jnp.broadcast_to(row, (total, 128)).reshape(nb, rows, 128)
    row_out[...] = jnp.sum(jnp.where(lane == sublane, pot[b], 0.0), axis=0, keepdims=True)[:, :rows]

    for role in range(2):
        for d in range(half):
            drain(data_buf.at[role], first_send.at[role, d], 2 if d else 1)
            drain(data_buf.at[role], on_send.at[role, d], 2)
        for d in range(half - 1, 1, -1):
            drain(data_buf.at[role], outer_send.at[role, d], 2)
        drain(outer_buf.at[role], outer_send.at[role, 0], 1)
        drain(noise_buf.at[role], noise_send.at[role], nb // 2 - 1)
    arrival(outer_send, 1, len(early))
    arrival(outer_send, half, len(late))
    drain(norm_b, small_send.at[0], nf - 1)
    drain(a_buf, small_send.at[1], nf - 1)
    drain(b_buf, small_send.at[2], nb - 1)
    drain(c_buf, small_send.at[3], nf - 1)
    for sem, first, count, blocks in groups:
        view = obuf.at[0, pl.ds(0, blocks), :, pl.ds(first, count)]
        pltpu.make_async_copy(view, view, out_send.at[sem]).wait()
        pltpu.make_async_copy(view, view, out_recv.at[sem]).wait()
    for c in kept:
        c.wait()


def place(targets, row, column, targets_out, row_out, column_out, sem):
    targets_out[...] = targets[...]
    row_out[...] = row[...]
    column_out[...] = column[...]


def solution(mesh):
    nb, nf = mesh.shape["batch"], mesh.shape["feat"]

    def per_device(noise, data):
        rows, width = noise.shape
        total, w = rows * nb, width // nb
        piece = total // nf
        targets, row, column = pl.pallas_call(
            functools.partial(kernel, nb, nf),
            out_shape=(
                jax.ShapeDtypeStruct((rows, width), jnp.bfloat16),
                jax.ShapeDtypeStruct((1, rows), jnp.float32),
                jax.ShapeDtypeStruct((1, total), jnp.float32),
            ),
            in_specs=[pl.BlockSpec(memory_space=pl.ANY)] * 2,
            out_specs=[pl.BlockSpec(memory_space=pltpu.VMEM)] * 3,
            scratch_shapes=[
                pltpu.VMEM((2, nb // 2, rows, w), jnp.bfloat16),
                pltpu.VMEM((2, nb, rows, w), jnp.bfloat16),
                pltpu.VMEM((2, nb, rows, w), jnp.bfloat16),
                pltpu.VMEM((2, total, w), jnp.bfloat16),
                pltpu.VMEM((2, total, w), jnp.bfloat16),
                pltpu.VMEM((2, rows, width), jnp.bfloat16),
                pltpu.VMEM((2, nb // 2, rows, w), jnp.bfloat16),
                pltpu.VMEM((2, nb // 2 - 2, rows, w), jnp.bfloat16),
                pltpu.VMEM((nb, rows, total), jnp.float32),
                pltpu.VMEM((nf, piece, total), jnp.float32),
                pltpu.VMEM((piece + 1, total), jnp.float32),
                pltpu.VMEM((nb, piece + 1, total), jnp.float32),
                pltpu.VMEM((piece, total), jnp.float32),
                pltpu.VMEM((nf, piece, total), jnp.float32),
                pltpu.VMEM((rows, 128), jnp.float32),
                pltpu.VMEM((nf, rows, 128), jnp.float32),
                pltpu.VMEM((nb, rows, 128), jnp.float32),
                pltpu.VMEM((nb, rows, total), jnp.float32),
                pltpu.SemaphoreType.DMA((8,)),
                pltpu.SemaphoreType.DMA((2, nb // 4 + 1)),
                pltpu.SemaphoreType.DMA((2, nb // 4 + 1)),
                pltpu.SemaphoreType.DMA((2, nb // 4)),
                pltpu.SemaphoreType.DMA((2, nb // 4)),
                pltpu.SemaphoreType.DMA((2,)),
                pltpu.SemaphoreType.DMA((2,)),
                pltpu.SemaphoreType.DMA((2, nb // 4)),
                pltpu.SemaphoreType.DMA((2, nb // 4)),
                pltpu.SemaphoreType.DMA((4,)),
                pltpu.SemaphoreType.DMA((4,)),
                pltpu.SemaphoreType.DMA((8,)),
                pltpu.SemaphoreType.DMA((8,)),
                pltpu.SemaphoreType.REGULAR((6,)),
            ],
            compiler_params=pltpu.CompilerParams(
                collective_id=0, has_side_effects=True, vmem_limit_bytes=52 * 2**20
            ),
        )(noise, data)
        inside = pl.BlockSpec(memory_space=pltpu.VMEM)
        targets, row, column = pl.pallas_call(
            place,
            out_shape=(
                jax.ShapeDtypeStruct((rows, width), jnp.bfloat16),
                jax.ShapeDtypeStruct((1, rows), jnp.float32),
                jax.ShapeDtypeStruct((1, total), jnp.float32),
            ),
            in_specs=[inside] * 3,
            out_specs=(inside, inside, inside),
            scratch_shapes=[pltpu.SemaphoreType.DMA],
            compiler_params=pltpu.CompilerParams(vmem_limit_bytes=52 * 2**20),
        )(targets, row, column)
        return targets, row.reshape(rows), column.reshape(total)

    return jax.shard_map(
        per_device,
        mesh=mesh,
        in_specs=(P("batch", "feat"), P("batch", "feat")),
        out_specs=(P("batch", "feat"), P("batch"), P()),
        check_vma=False,
    )
```

```python
import functools
import math

import jax
import jax.numpy as jnp
from jax import lax
from jax.experimental import pallas as pl
from jax.experimental.pallas import tpu as pltpu
from jax.sharding import PartitionSpec as P

ITERS = 3
SHARED = 7
EARLY = 2
MESH = pl.DeviceIdType.MESH


def lse(values, axis):
    top = jnp.max(values, axis=axis, keepdims=True)
    return top + jnp.log(jnp.sum(jnp.exp(values - top), axis=axis, keepdims=True))


def plane_order(side):
    steps = [(y, x) for y in range(side) for x in range(side) if y or x]
    return sorted(steps, key=lambda s: -min(s[0], side - s[0]) - min(s[1], side - s[1]))


def far_first(count):
    return sorted(range(1, count), key=lambda k: (-min(k, count - k), k))


def kernel(
    nb, nf, noise, data, out, row_out, col_out,
    noise_buf, data_buf, outer_buf, full, outer_full, local_buf, obuf, outer_obuf,
    part, a_buf, own, b_buf, done, c_buf, norm_own, norm_b, pot, wbuf,
    local_sem, outer_send, outer_recv, first_send, first_recv, noise_send, noise_recv, on_send, on_recv,
    small_send, small_recv, out_send, out_recv, arrived,
):
    rows, width = noise.shape
    w = width // nb
    total = rows * nb
    piece = total // nf
    features = width * nf
    root = math.sqrt(features)
    log_count = math.log(total)
    half = nb // 4
    shared = w * SHARED // 8
    b, f = lax.axis_index("batch"), lax.axis_index("feat")
    core = lax.rem(b, 2)
    sibling = b + 1 - 2 * core
    side = math.isqrt(nf)
    b_order, f_order = far_first(nb), plane_order(side)
    fy, fx = f // side, lax.rem(f, side)

    def at(t):
        return dict(device_id=(t, f), device_id_type=MESH)

    def in_column(k):
        return at(lax.rem(b + k, nb))

    def place_at(y, x):
        return lax.rem(fy + y + side, side) * side + lax.rem(fx + x + side, side)

    def in_grid(y, x):
        return dict(device_id=(b, place_at(y, x)), device_id_type=MESH)

    def in_plane(k):
        return in_grid(*k)

    def drain(ref, sem, count):
        view = ref.at[pl.ds(0, count)]
        pltpu.make_async_copy(view, view, sem).wait()

    def wrap(t):
        return lax.rem(t + 2 * nb, nb)

    def pair(device):
        return pl.ds(pl.multiple_of(wrap(device) // 2 * 2, 2), 2)

    def columns_of(slice_at, q=0, n=w):
        return pl.ds(pl.multiple_of(slice_at * w + q, math.gcd(w, q)), n)

    def step_of(role):
        return 2 if role == 0 else -2

    def slice_for(role, member):
        return wrap(member - 2 * role)

    def outer_slice(role, device):
        return slice_for(role, wrap(device + step_of(role)))

    def remote(source, target, send, recv, device):
        pltpu.make_async_remote_copy(
            src_ref=source, dst_ref=target, send_sem=send, recv_sem=recv, **device
        ).start()

    beside = [in_column(2), in_column(nb - 2)]
    diagonal = [at(wrap(sibling + 2)), at(wrap(sibling - 2))]
    row_beside = [in_grid(0, 1), in_grid(0, -1)]
    column_beside = [in_grid(1, 0), in_grid(-1, 0)]
    barrier = pltpu.get_barrier_semaphore()
    near = beside + diagonal + [at(sibling)] + row_beside + column_beside
    for device in near:
        pl.semaphore_signal(barrier, inc=1, **device)
    pl.semaphore_wait(barrier, len(near))

    def tell(devices, which):
        for device in devices:
            pl.semaphore_signal(arrived.at[which], inc=1, **device)

    tell(beside, 0)
    tell(row_beside, 3)

    for role in range(2):
        for member in (b, sibling):
            remote(
                data.at[:, columns_of(slice_for(role, member))], data_buf.at[1 - role, b],
                on_send.at[role, 0], on_recv.at[1 - role, 0], at(wrap(member + step_of(role))),
            )
    def send_data(d):
        for role in range(2):
            for member in [sibling] if d == 0 else [
                wrap(b + step_of(role) * d), wrap(sibling + step_of(role) * d)
            ]:
                source = data.at[:, columns_of(slice_for(role, member))]
                if d > 1:
                    remote(
                        source, outer_buf.at[role, b],
                        first_send.at[role, d], outer_recv.at[role, d], at(wrap(member - step_of(role))),
                    )
                else:
                    remote(
                        source, data_buf.at[role, b], first_send.at[role, d], first_recv.at[role, d], at(member)
                    )
    send_data(2)
    pl.semaphore_wait(arrived.at[0], 2)
    tell(beside, 1)
    for d in (3, 1, 0):
        send_data(d)
    locals_ = []
    for role in range(2):
        s = columns_of(slice_for(role, b))
        locals_.append(pltpu.make_async_copy(data.at[:, s], data_buf.at[role, b], local_sem.at[role]))
        locals_.append(pltpu.make_async_copy(noise.at[:, s], noise_buf.at[role, core], local_sem.at[2 + role]))
        s = columns_of(outer_slice(role, b))
        locals_.append(pltpu.make_async_copy(data.at[:, s], outer_buf.at[role, b], local_sem.at[6 + role]))
    locals_.append(pltpu.make_async_copy(noise, local_buf.at[0], local_sem.at[4]))
    locals_.append(pltpu.make_async_copy(data, local_buf.at[1], local_sem.at[5]))
    for c in locals_:
        c.start()
    for role in range(2):
        remote(
            data.at[:, columns_of(outer_slice(role, sibling))], outer_buf.at[role, b],
            outer_send.at[role, 0], outer_recv.at[role, 0], at(sibling),
        )

    def send_noise(distances):
        for d in distances:
            for role in range(2):
                for member in [sibling] if d == 0 else [
                    wrap(b + step_of(role) * d), wrap(sibling + step_of(role) * d)
                ]:
                    remote(
                        noise.at[:, columns_of(slice_for(role, member))], noise_buf.at[role, 2 * d + core],
                        noise_send.at[role], noise_recv.at[role], at(member),
                    )

    pl.semaphore_wait(arrived.at[3], 2)
    tell(column_beside, 4)
    pl.semaphore_wait(arrived.at[1], 2)
    tell(beside, 2)
    send_noise([half - 1])
    pl.semaphore_wait(arrived.at[4], 2)
    tell(column_beside, 5)
    pl.semaphore_wait(arrived.at[2], 2)
    pl.semaphore_wait(arrived.at[5], 2)
    for c in locals_:
        c.wait()

    def exchange(src_of, buf, slot, partner, order, sem):
        for k in order:
            remote(src_of(k), buf.at[slot], small_send.at[sem], small_recv.at[sem], partner(k))

    chunk = min(2048, width)
    sums = []
    for i in range(2):
        def add(step, acc, i=i):
            v = local_buf[i, :, pl.ds(pl.multiple_of(step * chunk, chunk), chunk)].astype(jnp.float32)
            v = v * v
            for q in range(chunk // 128):
                acc = acc + v[:, q * 128:(q + 1) * 128]
            return acc
        acc = lax.fori_loop(0, width // chunk, add, jnp.zeros((rows, 128), jnp.float32))
        sums.append(jnp.sum(acc, axis=1, keepdims=True))
    lane = lax.broadcasted_iota(jnp.int32, (rows, 128), 1)
    sublane = lax.broadcasted_iota(jnp.int32, (rows, 128), 0)
    norm_own[...] = jnp.where(lane < 64, sums[0], sums[1])
    norm_b[f] = norm_own[...]
    exchange(lambda k: norm_own, norm_b, f, in_plane, f_order, 0)

    def onward(d):
        for role in range(2):
            drain(data_buf.at[role], first_recv.at[role, d], 2)
            block = pair(b - step_of(role) * d)
            remote(
                data_buf.at[role, block], data_buf.at[1 - role, block],
                on_send.at[role, d], on_recv.at[1 - role, d], at(wrap(b + step_of(role))),
            )

    for d in range(half - 1, 1, -1):
        for role in range(2):
            drain(outer_buf.at[role], outer_recv.at[role, d], 2)
            block = pair(b - step_of(role) * (d - 1))
            remote(
                outer_buf.at[role, block], data_buf.at[role, block],
                outer_send.at[role, d], first_recv.at[role, d], at(wrap(b + step_of(role))),
            )
    onward(1)
    send_noise(range(half - 2, 1, -1))
    for d in range(half - 1, 1, -1):
        onward(d)
    send_noise([1, 0])

    drain(norm_b, small_recv.at[0], nf - 1)
    norms = jnp.sum(norm_b[...], axis=0)
    picked = jnp.where(lane == sublane, norms[:, :1], jnp.where(lane == sublane + rows, norms[:, 64:65], 0.0))
    own[piece:, :] = jnp.sum(picked, axis=0, keepdims=True)

    for role in range(2):
        drain(data_buf.at[role], first_recv.at[role, 0], 1)
        for d in range(half):
            drain(data_buf.at[role], on_recv.at[role, d], 2)
    def share(offsets, sem, first=0, count=shared):
        here = pl.ds(first, count)
        for d in offsets:
            for role in range(2):
                block = pair(b + step_of(role) * d)
                remote(
                    data_buf.at[role, block, :, here], outer_buf.at[role, block, :, here],
                    outer_send.at[role, sem], outer_recv.at[role, sem], at(wrap(b - step_of(role))),
                )

    offsets = list(range(half + 1))
    early, late = offsets[:EARLY], offsets[EARLY:]
    share(early, 1)
    share(late[:1], half, 0, shared // 2)

    chunk = min(1024, w)
    for role in range(2):
        for q in range(w // chunk):
            columns = pl.ds(q * chunk, chunk)
            full[role, :, columns] = (
                data_buf[role, :, :, columns].astype(jnp.float32).reshape(total, chunk).astype(jnp.bfloat16)
            )
    for role in range(2):
        drain(noise_buf.at[role], noise_recv.at[role], nb // 2 - 1)

    served = total // 2
    accs = [jnp.zeros((served, total), jnp.float32)] * 2
    chunk = min(1024, w)
    for q in range(w // chunk):
        columns = pl.ds(q * chunk, chunk)
        for role in range(2):
            left = noise_buf[role, :, :, columns].astype(jnp.float32).reshape(served, chunk).astype(jnp.bfloat16)
            accs[role] = accs[role] + lax.dot_general(
                left, full[role, :, columns], (((1,), (1,)), ((), ())), preferred_element_type=jnp.float32
            )
    for role in range(2):
        acc = accs[role].reshape(half, 2, rows, total)
        for d in range(half):
            block = pair(b - step_of(role) * d)
            if role and not d:
                part[block] = part[block] + acc[d]
            else:
                part[block] = acc[d]
    part[pair(b + nb // 2)] = jnp.zeros((2, rows, total), jnp.float32)

    part_of = part.reshape(nf, piece, total) if piece != rows else part
    a_buf[f] = part_of[f]
    exchange(lambda k: part_of.at[place_at(*k)], a_buf, f, in_plane, f_order, 1)
    drain(a_buf, small_recv.at[1], nf - 1)
    own[:piece, :] = jnp.sum(a_buf[...], axis=0)
    b_buf[b] = own[...]
    exchange(lambda k: own, b_buf, b, in_column, b_order, 2)
    share(late[:1], half, shared // 2, shared // 2)
    share(late[1:], half)

    def outer_pairs(devices, roles=(0, 1)):
        for role in roles:
            for device in devices(role):
                block = pair(device)
                at_row = pl.ds(pl.multiple_of(wrap(device) // 2 * (2 * rows), 2 * rows), 2 * rows)
                outer_full[role, at_row, :shared] = (
                    outer_buf[role, block, :, :shared].astype(jnp.float32)
                    .reshape(2 * rows, shared).astype(jnp.bfloat16)
                )

    def arrival(kind, sem, count, roles=(0, 1)):
        for role in roles:
            view = outer_buf.at[role, pl.ds(0, 2 * count), :, pl.ds(0, shared)]
            pltpu.make_async_copy(view, view, kind.at[role, sem]).wait()

    for role in range(2):
        drain(outer_buf.at[role], outer_recv.at[role, 0], 1)
    outer_pairs(lambda role: [b - step_of(role) * d for d in range(half - 1)])
    drain(b_buf, small_recv.at[2], nb - 1)
    done[...] = jnp.sum(b_buf[:, :piece, :], axis=0)
    c_buf[f] = done[...]
    exchange(lambda k: done, c_buf, f, in_plane, f_order, 3)
    norms = jnp.broadcast_to(b_buf[:, piece:, :], (nb, rows, 128))
    noise_norm = jnp.sum(jnp.where(lane == sublane, norms, 0.0), axis=2, keepdims=True).reshape(total, 1)
    data_norm = jnp.sum(jnp.where(lane == sublane + rows, norms, 0.0), axis=2, keepdims=True).reshape(total, 1)
    data_norm = jnp.transpose(jnp.broadcast_to(data_norm, (total, 128)))[:1, :]
    arrival(outer_recv, 1, len(early))
    outer_pairs(lambda role: [b + step_of(role) * (d + 1) for d in early])
    drain(c_buf, small_recv.at[3], nf - 1)
    cross = c_buf[...].reshape(total, total)

    scores = (2.0 * cross - noise_norm - data_norm) / root + 2.0 * root
    column = jnp.zeros((1, total), jnp.float32)
    for _ in range(ITERS):
        row = -log_count - lse(scores + column, 1)
        column = -log_count - lse(scores + row, 0)
    plan = jnp.exp(scores + row + column)
    weights = plan / jnp.sum(plan, axis=1, keepdims=True)
    wbuf[...] = weights.reshape(nb, rows, total)

    step = math.gcd(512, shared)
    kept = []

    def targets(chips, role, values, buf, first, count):
        blocks = []
        for d in chips:
            blocks += [wrap(sibling - step_of(role) * d), wrap(b - step_of(role) * d)]
        chosen = jnp.concatenate([wbuf[t] for t in blocks], axis=0).astype(jnp.bfloat16)
        for q in range(first, first + count, step):
            summed = jnp.dot(chosen, values[role, :, q:q + step], preferred_element_type=jnp.float32)
            buf[role, :len(blocks), :, q:q + step] = summed.reshape(len(blocks), rows, step).astype(jnp.bfloat16)

    def to_own(buf, role, place, slice_at, first, count, sem):
        where = columns_of(slice_at, first, count)
        remote(
            buf.at[role, place, :, pl.ds(first, count)], out.at[:, where],
            out_send.at[sem], out_recv.at[sem], at(sibling),
        )
        c = pltpu.make_async_copy(
            buf.at[role, place + 1, :, pl.ds(first, count)], out.at[:, where], local_sem.at[sem]
        )
        c.start()
        kept.append(c)

    def to_chips(chips, buf, slice_of, first, count, sem, roles):
        for q in range(nb // 2):
            for role in roles[::-1]:
                d = lax.rem((b // 2 - q if role == 0 else q - b // 2) + nb, nb // 2)

                @pl.when((d >= max(chips[-1], 1)) & (d <= chips[0]))
                def _(q=q, role=role, d=d):
                    where = columns_of(slice_of(role, b), first, count)
                    for i, t in enumerate((2 * q + 1 - core, 2 * q + core)):
                        place = 2 * (chips[0] - d) + i
                        remote(
                            buf.at[role, place, :, pl.ds(first, count)], out.at[:, where],
                            out_send.at[sem + role], out_recv.at[sem + role], at(t),
                        )

    far = list(range(half - 1, -1, -1))
    for role in range(2):
        targets(far, role, full, obuf, shared, w - shared)
    to_chips(far, obuf, slice_for, shared, w - shared, 0, (0, 1))
    for role in range(2):
        arrival(outer_recv, half, len(late), (role,))
        outer_pairs(lambda role: [b + step_of(role) * (d + 1) for d in late], (role,))
        targets(far[1:], role, outer_full, outer_obuf, 0, shared)
        to_chips(far[1:], outer_obuf, outer_slice, 0, shared, 4, (role,))
    for role in range(2):
        to_own(outer_obuf, role, nb // 2 - 4, outer_slice(role, b), 0, shared, 4 + role)
        to_own(obuf, role, nb // 2 - 2, slice_for(role, b), shared, w - shared, role)
        targets([0], role, full, obuf, 0, shared)
        to_own(obuf, role, 0, slice_for(role, b), 0, shared, 2 + role)
    groups = [
        (role + sem, first, count, blocks)
        for role in range(2)
        for sem, first, count, blocks in (
            (0, shared, w - shared, nb // 2 - 1), (2, 0, shared, 1), (4, 0, shared, nb // 2 - 3)
        )
    ]

    col_out[...] = column
    pot[...] = jnp.broadcast_to(row, (total, 128)).reshape(nb, rows, 128)
    row_out[...] = jnp.sum(jnp.where(lane == sublane, pot[b], 0.0), axis=0, keepdims=True)[:, :rows]

    for role in range(2):
        for d in range(half):
            drain(data_buf.at[role], first_send.at[role, d], 2 if d else 1)
            drain(data_buf.at[role], on_send.at[role, d], 2)
        for d in range(half - 1, 1, -1):
            drain(data_buf.at[role], outer_send.at[role, d], 2)
        drain(outer_buf.at[role], outer_send.at[role, 0], 1)
        drain(noise_buf.at[role], noise_send.at[role], nb // 2 - 1)
    arrival(outer_send, 1, len(early))
    arrival(outer_send, half, len(late))
    drain(norm_b, small_send.at[0], nf - 1)
    drain(a_buf, small_send.at[1], nf - 1)
    drain(b_buf, small_send.at[2], nb - 1)
    drain(c_buf, small_send.at[3], nf - 1)
    for sem, first, count, blocks in groups:
        view = obuf.at[0, pl.ds(0, blocks), :, pl.ds(first, count)]
        pltpu.make_async_copy(view, view, out_send.at[sem]).wait()
        pltpu.make_async_copy(view, view, out_recv.at[sem]).wait()
    for c in kept:
        c.wait()


def place(targets, row, column, targets_out, row_out, column_out, sem):
    n = targets_out.shape[1]
    here = pl.ds(pl.multiple_of(pl.program_id(0) * n, n), n)
    targets_out[...] = targets[:, here]
    row_out[...] = row[...]
    column_out[...] = column[...]


def solution(mesh):
    nb, nf = mesh.shape["batch"], mesh.shape["feat"]

    def per_device(noise, data):
        rows, width = noise.shape
        total, w = rows * nb, width // nb
        piece = total // nf
        targets, row, column = pl.pallas_call(
            functools.partial(kernel, nb, nf),
            out_shape=(
                jax.ShapeDtypeStruct((rows, width), jnp.bfloat16),
                jax.ShapeDtypeStruct((1, rows), jnp.float32),
                jax.ShapeDtypeStruct((1, total), jnp.float32),
            ),
            in_specs=[pl.BlockSpec(memory_space=pl.ANY)] * 2,
            out_specs=[pl.BlockSpec(memory_space=pltpu.VMEM)] * 3,
            scratch_shapes=[
                pltpu.VMEM((2, nb // 2, rows, w), jnp.bfloat16),
                pltpu.VMEM((2, nb, rows, w), jnp.bfloat16),
                pltpu.VMEM((2, nb, rows, w), jnp.bfloat16),
                pltpu.VMEM((2, total, w), jnp.bfloat16),
                pltpu.VMEM((2, total, w), jnp.bfloat16),
                pltpu.VMEM((2, rows, width), jnp.bfloat16),
                pltpu.VMEM((2, nb // 2, rows, w), jnp.bfloat16),
                pltpu.VMEM((2, nb // 2 - 2, rows, w), jnp.bfloat16),
                pltpu.VMEM((nb, rows, total), jnp.float32),
                pltpu.VMEM((nf, piece, total), jnp.float32),
                pltpu.VMEM((piece + 1, total), jnp.float32),
                pltpu.VMEM((nb, piece + 1, total), jnp.float32),
                pltpu.VMEM((piece, total), jnp.float32),
                pltpu.VMEM((nf, piece, total), jnp.float32),
                pltpu.VMEM((rows, 128), jnp.float32),
                pltpu.VMEM((nf, rows, 128), jnp.float32),
                pltpu.VMEM((nb, rows, 128), jnp.float32),
                pltpu.VMEM((nb, rows, total), jnp.float32),
                pltpu.SemaphoreType.DMA((8,)),
                pltpu.SemaphoreType.DMA((2, nb // 4 + 1)),
                pltpu.SemaphoreType.DMA((2, nb // 4 + 1)),
                pltpu.SemaphoreType.DMA((2, nb // 4)),
                pltpu.SemaphoreType.DMA((2, nb // 4)),
                pltpu.SemaphoreType.DMA((2,)),
                pltpu.SemaphoreType.DMA((2,)),
                pltpu.SemaphoreType.DMA((2, nb // 4)),
                pltpu.SemaphoreType.DMA((2, nb // 4)),
                pltpu.SemaphoreType.DMA((4,)),
                pltpu.SemaphoreType.DMA((4,)),
                pltpu.SemaphoreType.DMA((8,)),
                pltpu.SemaphoreType.DMA((8,)),
                pltpu.SemaphoreType.REGULAR((6,)),
            ],
            compiler_params=pltpu.CompilerParams(
                collective_id=0, has_side_effects=True, vmem_limit_bytes=52 * 2**20
            ),
        )(noise, data)
        inside = pl.BlockSpec(memory_space=pltpu.VMEM)
        targets, row, column = pl.pallas_call(
            place,
            out_shape=(
                jax.ShapeDtypeStruct((rows, width), jnp.bfloat16),
                jax.ShapeDtypeStruct((1, rows), jnp.float32),
                jax.ShapeDtypeStruct((1, total), jnp.float32),
            ),
            in_specs=[inside] * 3,
            grid=(2,),
            out_specs=(pl.BlockSpec((rows, width // 2), lambda i: (0, i)), inside, inside),
            scratch_shapes=[pltpu.SemaphoreType.DMA],
            compiler_params=pltpu.CompilerParams(vmem_limit_bytes=52 * 2**20),
        )(targets, row, column)
        return targets, row.reshape(rows), column.reshape(total)

    return jax.shard_map(
        per_device,
        mesh=mesh,
        in_specs=(P("batch", "feat"), P("batch", "feat")),
        out_specs=(P("batch", "feat"), P("batch"), P()),
        check_vma=False,
    )
```
